256 devices in a mesh: dp: 16 (over x, y_hi, core), seq: 16 (over z, y_lo).
Axes of the slice: x: 4, y: 4 (y_hi: 2, y_lo: 2; y = y_hi * 2 + y_lo), z: 8, core: 2. Of those that a mesh axis runs over, the one named last changes fastest.
Arguments:
- coarse: bfloat16 [16, 4096, 1024], P('dp', 'seq'), may hold values from -6 to 6
- skip: bfloat16 [16, 8192, 768], P('dp', 'seq'), may hold values from -6 to 6
- conv_weight: bfloat16 [5, 1024, 768], replicated, may hold values from -0.078125 to 0.078125
- donor_weight: bfloat16 [768, 768], replicated, may hold values from -0.21875 to 0.21875
- acceptor_weight: bfloat16 [768, 768], replicated, may hold values from -0.21875 to 0.21875
- other_grad: bfloat16 [16, 8192, 768], P('dp', 'seq'), may hold values from -4 to 4
- score_grad: float32 [16, 1024], P('dp', 'seq'), may hold values from -16 to 16
- donor_pos: int32 [16, 1024], P('dp', 'seq'), may hold values from 0 to 511
- acceptor_pos: int32 [16, 1024], P('dp', 'seq'), may hold values from 0 to 8191, as said below
- pair_mask: int32 [16, 1024], P('dp', 'seq'), may hold values 0 or 1
Outputs:
- scores: float32 [16, 1024], P('dp', 'seq')
- coarse_grad: bfloat16 [16, 4096, 1024], P('dp', 'seq')
- donor_weight_grad: float32 [768, 768], P('seq')
- acceptor_weight_grad: float32 [768, 768], P('seq')
The draws below stay inside these ranges and needn't reach their ends.
Inputs may be any that keep to these rules, and one draw needn't show every extreme that they name: Position in the whole sample. Among the 64 slots held by one shard of a sample, at most 8 have their acceptor on any one shard (shard = acceptor_pos // 512); in every sample some shard is named by exactly 8 slots of every shard.
All inputs are finite; a program needn't handle non-finite values. No bound on the sum of `pair_mask` on one device may be relied on, other than what follows from the above.
Results may differ from the reference program's by a relative error of at most 0.013.
Values may be sent and summed in bfloat16 or wider, within the bound.
A program may use at most 128 MiB of HBM per device.

```python
import math
import jax
import jax.numpy as jnp
from jax import lax

C_IN = 1024
C_OUT = 768
EMB = 768
TAPS = 5
ACAP = 8
ROWS_DEV = 512
LENGTH = 8192
COARSE_LEN = 4096
JCAP = 64
JUNCTIONS = 1024
BATCH = 16
N_SEQ = 16


def draw_acceptor_pos(key, part):
    batch_keys = jax.random.split(jax.random.fold_in(key, 7), BATCH)

    def one_batch(batch_key):
        hottest = jax.random.randint(jax.random.fold_in(batch_key, 1), (), 0, N_SEQ)
        shard_keys = jax.random.split(jax.random.fold_in(batch_key, 2), N_SEQ)

        def one_shard(shard_key):
            first_key, second_key, third_key = jax.random.split(shard_key, 3)
            tickets = jax.random.permutation(first_key, (N_SEQ - 1) * ACAP)[:JCAP - ACAP]
            others = (hottest + 1 + tickets // ACAP) % N_SEQ
            owners = jnp.concatenate([jnp.full((ACAP,), hottest, jnp.int32), others.astype(jnp.int32)])
            owners = jax.random.permutation(second_key, owners)
            offsets = jax.random.randint(third_key, (JCAP,), 0, ROWS_DEV)
            return owners * ROWS_DEV + offsets
        return jax.vmap(one_shard)(shard_keys).reshape(-1)
    return jax.vmap(one_batch)(batch_keys).astype(jnp.int32)


def with_ends(array, rng, smallest, top_value):
    place = [jax.random.randint(jax.random.fold_in(rng, axis), (), 0, length) for axis, length in enumerate(array.shape)]
    main_axis = array.shape.index(max(array.shape))
    next_to = place[:main_axis] + [(place[main_axis] + 1) % array.shape[main_axis]] + place[main_axis + 1:]
    return array.at[tuple(place)].set(smallest).at[tuple(next_to)].set(top_value)


def block_levels(own_key, dims, pieces, smallest, largest):
    factor_of, own = 1.0, jax.random.fold_in(own_key, 6)
    for position, blocks in pieces:
        draws = jnp.exp(jax.random.uniform(jax.random.fold_in(own, position), (blocks,), jnp.float32, smallest / len(pieces), largest / len(pieces)))
        factor_of = factor_of * jnp.repeat(draws, dims[position] // blocks).reshape([-1 if axis == position else 1 for axis in range(len(dims))])
    return factor_of


def normal_values(stream_key, shape, width, most, pieces=(), held_as=jnp.bfloat16):
    loudness = block_levels(stream_key, shape, pieces, -0.22, 0.18) if pieces else 1.0
    array = jax.random.normal(stream_key, shape, jnp.float32) * width * loudness
    return jnp.minimum(jnp.maximum(array, -most), most).astype(held_as)


def setup_inputs(seed: int = 0) -> dict:
    key_of = jax.random.split(jax.random.key(seed), 11)
    coarse = normal_values(key_of[0], (BATCH, COARSE_LEN, C_IN), 1.0, 6.0, ((0, 16), (1, 16)))
    skip = normal_values(key_of[1], (BATCH, LENGTH, C_OUT), 1.0, 6.0, ((0, 16), (1, 16)))
    conv_weight = normal_values(key_of[2], (TAPS, C_IN, C_OUT), (TAPS * C_IN) ** -0.5, 0.078125)
    donor_weight = normal_values(key_of[3], (C_OUT, EMB), C_OUT ** -0.5, 0.21875)
    acceptor_weight = normal_values(key_of[4], (C_OUT, EMB), C_OUT ** -0.5, 0.21875)
    other_grad = normal_values(key_of[5], (BATCH, LENGTH, C_OUT), 0.3, 4.0, ((0, 16), (1, 16)))
    score_grad = normal_values(key_of[6], (BATCH, JUNCTIONS), 3.0, 16.0, ((0, 16), (1, 16)), jnp.float32)
    donor_pos = with_ends(jax.random.randint(key_of[7], (BATCH, JUNCTIONS), 0, ROWS_DEV), jax.random.fold_in(key_of[7], 1), 0, ROWS_DEV - 1).astype(jnp.int32)
    acceptor_pos = draw_acceptor_pos(jax.random.fold_in(key_of[10], 71), 0)
    pair_mask = with_ends((jax.random.randint(key_of[9], (BATCH, JUNCTIONS), 0, 4) < 3).astype(jnp.int32), jax.random.fold_in(key_of[9], 1), 0, 1)
    return dict(coarse=coarse, skip=skip, conv_weight=conv_weight, donor_weight=donor_weight, acceptor_weight=acceptor_weight, other_grad=other_grad, score_grad=score_grad, donor_pos=donor_pos, acceptor_pos=acceptor_pos, pair_mask=pair_mask)


def activate(values):
    return jax.nn.gelu(values, approximate=True)

def one_sample(conv_weight, donor_weight, acceptor_weight, inputs):
    coarse_row, skip_row, other_row, score_row, donor_row, acceptor_row, mask_row = inputs
    inverse_root = 1.0 / math.sqrt(EMB)
    upsampled = jnp.pad(jnp.repeat(coarse_row, 2, axis=0), ((2, 2), (0, 0)))
    preact = skip_row.astype(jnp.float32)
    for shift_index in range(TAPS):
        preact = preact + jnp.dot(upsampled[shift_index:shift_index + LENGTH], conv_weight[shift_index], preferred_element_type=jnp.float32)
    activated = activate(preact).astype(jnp.bfloat16)
    shard_of = jnp.arange(JUNCTIONS, dtype=jnp.int32) // JCAP
    donor_global = (shard_of * ROWS_DEV + donor_row).astype(jnp.int32)
    acceptor_global = acceptor_row.astype(jnp.int32)
    donor_act = activated[donor_global]
    acceptor_act = activated[acceptor_global]
    donor_emb = jnp.dot(donor_act, donor_weight, preferred_element_type=jnp.float32).astype(jnp.bfloat16)
    acceptor_emb = jnp.dot(acceptor_act, acceptor_weight, preferred_element_type=jnp.float32).astype(jnp.bfloat16)
    mask_float = mask_row.astype(jnp.float32)
    scores = mask_float * lax.optimization_barrier(jnp.sum(donor_emb.astype(jnp.float32) * acceptor_emb.astype(jnp.float32), axis=1)) * inverse_root
    weighted = score_row * mask_float
    donor_emb_grad = (weighted[:, None] * acceptor_emb.astype(jnp.float32) * inverse_root).astype(jnp.bfloat16)
    acceptor_emb_grad = (weighted[:, None] * donor_emb.astype(jnp.float32) * inverse_root).astype(jnp.bfloat16)
    act_grad = other_row.astype(jnp.float32)
    act_grad = act_grad.at[donor_global].add(jnp.dot(donor_emb_grad, donor_weight.T, preferred_element_type=jnp.float32))
    act_grad = act_grad.at[acceptor_global].add(jnp.dot(acceptor_emb_grad, acceptor_weight.T, preferred_element_type=jnp.float32))
    pull = jax.vjp(activate, preact)[1]
    preact_grad = pull(act_grad)[0].astype(jnp.bfloat16)
    padded_grad = jnp.pad(preact_grad, ((2, 2), (0, 0)))
    upsampled_grad = jnp.zeros((LENGTH, C_IN), jnp.float32)
    for shift_index in range(TAPS):
        begin = 4 - shift_index
        upsampled_grad = upsampled_grad + jnp.dot(padded_grad[begin:begin + LENGTH], conv_weight[shift_index].T, preferred_element_type=jnp.float32)
    coarse_grad = upsampled_grad.reshape(LENGTH // 2, 2, C_IN).sum(axis=1).astype(jnp.bfloat16)
    donor_term = jnp.dot(donor_act.T, donor_emb_grad, preferred_element_type=jnp.float32)
    acceptor_term = jnp.dot(acceptor_act.T, acceptor_emb_grad, preferred_element_type=jnp.float32)
    return (scores, coarse_grad, donor_term, acceptor_term)

def reference(coarse, skip, conv_weight, donor_weight, acceptor_weight, other_grad, score_grad, donor_pos, acceptor_pos, pair_mask):

    def mapped(inputs):
        return one_sample(conv_weight, donor_weight, acceptor_weight, inputs)
    scores, coarse_grad, donor_terms, acceptor_terms = lax.map(mapped, (coarse, skip, other_grad, score_grad, donor_pos, acceptor_pos, pair_mask))
    donor_weight_grad = lax.optimization_barrier(jnp.sum(donor_terms, axis=0)) / BATCH
    acceptor_weight_grad = lax.optimization_barrier(jnp.sum(acceptor_terms, axis=0)) / BATCH
    return (scores, coarse_grad, donor_weight_grad, acceptor_weight_grad)
```

```python
import math

import jax
import jax.numpy as jnp
from jax import lax
from jax.experimental import pallas as pl
from jax.experimental.pallas import tpu as pltpu
from jax.sharding import PartitionSpec as P

MESH = pl.DeviceIdType.MESH
F32, BF16, I32 = jnp.float32, jnp.bfloat16, jnp.int32
N_X, N_Y, N_Z = 4, 4, 8
N_DP, N_SEQ = 16, 16
COARSE, FINE, C_IN, C_OUT, EMB = 256, 512, 1024, 768, 768
EXT = COARSE + 16
TAPS, ACAP, SLOTS = 5, 8, 64
CAP = N_SEQ * ACAP
TILE = 256
HALF = 384
BLOCK = 256
ROWS_SEQ = C_OUT // N_SEQ
INV_ROOT = 1.0 / math.sqrt(EMB)
K0 = math.sqrt(2.0 / math.pi)
K1 = 0.044715


def dot(a, b):
    return jnp.dot(a, b, preferred_element_type=F32)


def dot_nt(a, b):
    return lax.dot_general(a, b, (((1,), (1,)), ((), ())), preferred_element_type=F32)


def dot_tn(a, b):
    return lax.dot_general(a, b, (((0,), (0,)), ((), ())), preferred_element_type=F32)


def one_hot(condition):
    return jnp.where(condition, 1.0, 0.0).astype(BF16)


def iota(shape, axis):
    return lax.broadcasted_iota(I32, shape, axis)


def as_column(row):
    return jnp.transpose(jnp.broadcast_to(row, (128, 128)))[:, 0:1]


def as_row(column):
    return jnp.transpose(jnp.broadcast_to(column, (128, 128)))[0:1, :]


def folded(row):
    return jnp.where(row < 0, -1, (row & 1) * COARSE + (row >> 1))


def pack(rows):
    cells = rows.reshape(N_SEQ, ACAP, EMB)
    return jnp.concatenate([cells[:, :, :HALF], cells[:, :, HALF:]], axis=1).astype(BF16)


def unpack(cells):
    wide = cells.astype(F32)
    both = jnp.concatenate([wide[:, :ACAP], wide[:, ACAP:]], axis=2)
    return both.reshape(CAP, EMB).astype(BF16)


def kernel(
    coarse, skip, conv_w, donor_w, acceptor_w, other, score_grad, donor_pos, acceptor_pos, mask,
    scores_out, coarse_out, donor_out, acceptor_out,
    w, wd, wa, c_ext, skip_in, other_in, skip_f, other_f, act, slope,
    halo_next, halo_prev, grad_next, grad_prev, grad_left, grad_right,
    pos_own, pos_all, a1_send, a1_recv, a2_send, a2_recv,
    pe, po, out_v, dact, dgrad, aact, agrad,
    f_act, f_grad, sum1, part2, sum2, part3, piece, pieces,
    load_sem, w_sem, out_sem, halo_ssem, halo_rsem, ghalo_ssem, ghalo_rsem,
    pos_ssem, pos_rsem, a1_ssem, a1_rsem, a2_ssem, a2_rsem,
    f_ssem, f_rsem, g_ssem, g_rsem, local_sem,
    s2_ssem, s2_rsem, s3_ssem, s3_rsem, ag_ssem, ag_rsem,
):
    dp, seq = lax.axis_index("dp"), lax.axis_index("seq")
    x, yh, core = dp // 4, (dp // 2) % 2, dp % 2
    z, yl = seq // 2, seq % 2
    y = yh * 2 + yl

    loads = [
        pltpu.make_async_copy(coarse.at[0], c_ext.at[pl.ds(0, COARSE)], load_sem.at[0]),
        pltpu.make_async_copy(skip.at[0], skip_in, load_sem.at[1]),
        pltpu.make_async_copy(donor_w, wd, load_sem.at[2]),
        pltpu.make_async_copy(acceptor_w, wa, load_sem.at[3]),
        pltpu.make_async_copy(other.at[0], other_in, load_sem.at[4]),
    ]

    def load_w(n):
        cols = pl.ds(pl.multiple_of(n * TILE, TILE), TILE)
        return pltpu.make_async_copy(conv_w.at[:, :, cols], w.at[:, :, cols], w_sem.at[n])

    loads[0].start()
    loads[1].start()
    for n in range(C_OUT // TILE):
        load_w(n).start()
    loads[2].start()
    loads[3].start()
    loads[4].start()

    halo_next[...] = jnp.zeros_like(halo_next)
    halo_prev[...] = jnp.zeros_like(halo_prev)
    grad_next[...] = jnp.zeros_like(grad_next)
    grad_prev[...] = jnp.zeros_like(grad_prev)
    own_row = jnp.concatenate([acceptor_pos[...], jnp.full((1, 64), -1, I32)], axis=1)
    pos_own[...] = jnp.broadcast_to(own_row, (8, 128))

    barrier = pltpu.get_barrier_semaphore()

    def greet_seq(i, carry):
        pl.semaphore_signal(barrier, inc=1, device_id=(dp, (seq + i) % N_SEQ), device_id_type=MESH)
        return carry

    def greet_dp(i, carry):
        other_dp = (dp + i) % N_DP
        pl.semaphore_signal(barrier, inc=1, device_id=(other_dp, seq), device_id_type=MESH)
        pl.semaphore_signal(
            barrier, inc=1, device_id=(other_dp, z * 2 + 1 - yl), device_id_type=MESH
        )
        return carry

    lax.fori_loop(1, N_SEQ, greet_seq, 0)
    lax.fori_loop(1, N_DP, greet_dp, 0)
    pl.semaphore_wait(barrier, N_SEQ - 1 + 2 * (N_DP - 1))

    loads[0].wait()

    def halo_left():
        return pltpu.make_async_remote_copy(
            c_ext.at[pl.ds(0, 16)], halo_next, halo_ssem.at[0], halo_rsem.at[0],
            device_id=(dp, (seq + N_SEQ - 1) % N_SEQ), device_id_type=MESH)

    def halo_right():
        return pltpu.make_async_remote_copy(
            c_ext.at[pl.ds(COARSE - 16, 16)], halo_prev, halo_ssem.at[1], halo_rsem.at[1],
            device_id=(dp, (seq + 1) % N_SEQ), device_id_type=MESH)

    @pl.when(seq > 0)
    def _():
        halo_left().start()

    @pl.when(seq < N_SEQ - 1)
    def _():
        halo_right().start()

    def pos_copy(i):
        return pltpu.make_async_remote_copy(
            pos_own, pos_all.at[seq], pos_ssem.at[i], pos_rsem.at[seq],
            device_id=(dp, (seq + i) % N_SEQ), device_id_type=MESH)

    def pos_start(i, carry):
        pos_copy(i).start()
        return carry

    lax.fori_loop(1, N_SEQ, pos_start, 0)
    pos_all[seq] = pos_own[...]

    loads[1].wait()
    at = iota((COARSE, FINE), 1)
    step2 = 2 * iota((COARSE, FINE), 0)
    even, odd = one_hot(at == step2), one_hot(at == step2 + 1)
    skip_f[pl.ds(0, COARSE)] = dot(even, skip_in[...]).astype(BF16)
    skip_f[pl.ds(COARSE, COARSE)] = dot(odd, skip_in[...]).astype(BF16)

    sub, lane = iota((128, 128), 0), iota((128, 128), 1)
    before = one_hot(sub < lane)
    place = sub % ACAP
    own = jnp.broadcast_to(own_row, (128, 128))
    own_hit = (own >> 9) == sub // ACAP
    own_rank = dot(one_hot(own_hit), before).astype(I32)
    to_served = jnp.where(own_hit & (own_rank == place), 1.0, 0.0)
    from_served = jnp.transpose(to_served)[:SLOTS].astype(BF16)
    to_served = to_served[:, :SLOTS].astype(BF16)
    pad = jnp.full((1, 64), -1, I32)
    donor_row = folded(jnp.concatenate([donor_pos[...], pad], axis=1))
    donor_column = as_column(donor_row.astype(F32)).astype(I32)[:SLOTS]
    from_donor = one_hot(iota((SLOTS, FINE), 1) == donor_column)
    to_donor = one_hot(iota((FINE, 128), 0) == donor_row)
    fpad = jnp.zeros((1, 64), F32)
    mask_column = as_column(jnp.concatenate([mask[...].astype(F32), fpad], axis=1))[:SLOTS]
    score_column = as_column(jnp.concatenate([score_grad[...], fpad], axis=1))[:SLOTS]
    weighted = score_column * mask_column

    @pl.when(seq < N_SEQ - 1)
    def _():
        halo_left().wait_recv()

    @pl.when(seq > 0)
    def _():
        halo_right().wait_recv()

    row16 = iota((16, C_IN), 0)
    c_ext[pl.ds(COARSE, 16)] = jnp.where(
        row16 == 0, halo_next[...].astype(F32),
        jnp.where(row16 == 15, halo_prev[...].astype(F32), 0.0),
    ).astype(BF16)

    def conv_tile(n, carry):
        load_w(n).wait()
        cols = pl.ds(pl.multiple_of(n * TILE, TILE), TILE)
        cells = c_ext[...]
        taps = [dot(cells, w[k, :, cols]) for k in range(TAPS)]
        even_sum = (
            pltpu.roll(taps[0] + taps[1], 1, 0) + taps[2] + taps[3] + pltpu.roll(taps[4], EXT - 1, 0)
        )
        odd_sum = (
            pltpu.roll(taps[0], 1, 0) + taps[1] + taps[2] + pltpu.roll(taps[3] + taps[4], EXT - 1, 0)
        )
        for part, total in ((0, even_sum), (1, odd_sum)):
            rows = pl.ds(part * COARSE, COARSE)
            v = total[:COARSE] + skip_f[rows, cols].astype(F32)
            square = v * v
            t = jnp.tanh(K0 * v * (1.0 + K1 * square))
            half = 0.5 * (1.0 + t)
            act[rows, cols] = (v * half).astype(BF16)
            slope[rows, cols] = half + 0.5 * v * (1.0 - t * t) * (K0 * (1.0 + 3.0 * K1 * square))
        return carry

    lax.fori_loop(0, C_OUT // TILE, conv_tile, 0)

    def pos_wait(i, carry):
        src = (seq + i) % N_SEQ
        pltpu.make_async_remote_copy(
            pos_own, pos_all.at[src], pos_ssem.at[i], pos_rsem.at[src],
            device_id=(dp, src), device_id_type=MESH).wait_recv()
        return carry

    lax.fori_loop(1, N_SEQ, pos_wait, 0)
    named = pos_all[...].reshape(CAP, 128)
    hit = (named >> 9) == seq
    rank = dot(one_hot(hit), before).astype(I32)
    chosen = jnp.where(hit & (rank == place), (named & (FINE - 1)) + 1, 0).astype(F32)
    served = jnp.sum(chosen, axis=1, keepdims=True).astype(I32) - 1
    served = folded(served)
    from_rows = one_hot(iota((CAP, FINE), 1) == served)
    served_row = as_row(served.astype(F32)).astype(I32)
    to_rows = one_hot(iota((FINE, CAP), 0) == served_row)
    a1_send[...] = pack(dot(from_rows, act[...]))

    def exchange(send, recv, ssem, rsem):
        def copy(i):
            peer = (seq + i) % N_SEQ
            return pltpu.make_async_remote_copy(
                send.at[peer], recv.at[seq], ssem.at[i], rsem.at[seq],
                device_id=(dp, peer), device_id_type=MESH)

        def start(i, carry):
            copy(i).start()
            return carry

        def wait(i, carry):
            src = (seq + i) % N_SEQ
            pltpu.make_async_remote_copy(
                send.at[src], recv.at[src], ssem.at[i], rsem.at[src],
                device_id=(dp, src), device_id_type=MESH).wait_recv()
            return carry

        def drain(i, carry):
            copy(i).wait_send()
            return carry

        return [lambda f=f: lax.fori_loop(1, N_SEQ, f, 0) for f in (start, wait, drain)]

    a1_start, a1_wait, a1_drain = exchange(a1_send, a1_recv, a1_ssem, a1_rsem)
    a2_start, a2_wait, a2_drain = exchange(a2_send, a2_recv, a2_ssem, a2_rsem)
    a1_start()
    a1_recv[seq] = a1_send[seq]

    loads[2].wait()
    loads[3].wait()
    donor_act = dot(from_donor, act[...]).astype(BF16)
    donor_emb = dot(donor_act, wd[...]).astype(BF16).astype(F32)
    acceptor_emb_grad = (weighted * donor_emb * INV_ROOT).astype(BF16)
    acceptor_rows = dot_nt(acceptor_emb_grad, wa[...]).astype(BF16)
    a2_send[...] = pack(dot(to_served, acceptor_rows))
    a2_start()
    a2_recv[seq] = a2_send[seq]
    dact[...] = donor_act
    agrad[...] = acceptor_emb_grad

    loads[4].wait()
    other_f[pl.ds(0, COARSE)] = dot(even, other_in[...]).astype(BF16)
    other_f[pl.ds(COARSE, COARSE)] = dot(odd, other_in[...]).astype(BF16)

    a1_wait()
    acceptor_act = dot(from_served, unpack(a1_recv[...])).astype(BF16)
    acceptor_emb = dot(acceptor_act, wa[...]).astype(BF16).astype(F32)
    score = mask_column * jnp.sum(donor_emb * acceptor_emb, axis=1, keepdims=True) * INV_ROOT
    score = jnp.concatenate([score, jnp.zeros((128 - SLOTS, 1), F32)], axis=0)
    scores_out[...] = as_row(score)[:, :SLOTS]
    donor_emb_grad = (weighted * acceptor_emb * INV_ROOT).astype(BF16)
    aact[...] = acceptor_act
    dgrad[...] = donor_emb_grad

    acts, grads = (dact, aact), (dgrad, agrad)

    def target(kind, p):
        if kind == 0:
            return (p * 4 + yh * 2, seq)
        return (x * 4 + (p // 2) * 2 + 1, z * 2 + p % 2)

    ring_at = (x, y)
    first = jnp.where(core == 0, x, y)
    second = jnp.where(core == 0, y, x)
    active = first < 3

    def factor_copies(kind, p, source):
        slot = kind * 3 + p
        cols = pl.ds(p * BLOCK, BLOCK)
        device = target(kind, p)
        return [
            pltpu.make_async_remote_copy(
                acts[kind], f_act.at[source], f_ssem.at[slot], f_rsem.at[source],
                device_id=device, device_id_type=MESH),
            pltpu.make_async_remote_copy(
                grads[kind].at[:, cols], f_grad.at[source], g_ssem.at[slot], g_rsem.at[source],
                device_id=device, device_id_type=MESH),
        ]

    for kind in range(2):
        source = ring_at[kind] * 2 + core
        for p in range(3):
            mine = (core == kind) & (ring_at[kind] == p)

            @pl.when(jnp.logical_not(mine))
            def _(kind=kind, p=p, source=source):
                for copy in factor_copies(kind, p, source):
                    copy.start()

            @pl.when(mine)
            def _(kind=kind, p=p, source=source):
                f_act[source] = acts[kind][...]
                f_grad[source] = grads[kind][:, p * BLOCK:(p + 1) * BLOCK]

    donor_rows = dot_nt(donor_emb_grad, wd[...]).astype(BF16)
    a2_wait()
    served_rows = unpack(a2_recv[...])

    def grad_of(rows):
        total = (
            other_f[rows].astype(F32)
            + dot(to_rows[rows.start:rows.start + rows.size], served_rows)
            + dot(to_donor[rows.start:rows.start + rows.size, :SLOTS], donor_rows)
        )
        return total * slope[rows]

    g_even = grad_of(pl.ds(0, COARSE))
    g_odd = grad_of(pl.ds(COARSE, COARSE))
    pair = g_even + g_odd
    pe[pl.ds(0, COARSE)] = pair.astype(BF16)
    grad_left[pl.ds(0, 16)] = pair[:16].astype(BF16)
    grad_left[pl.ds(16, 16)] = g_even[:16].astype(BF16)
    grad_right[pl.ds(0, 16)] = pair[COARSE - 16:].astype(BF16)
    grad_right[pl.ds(16, 16)] = g_odd[COARSE - 16:].astype(BF16)

    def ghalo_left():
        return pltpu.make_async_remote_copy(
            grad_left, grad_next, ghalo_ssem.at[0], ghalo_rsem.at[0],
            device_id=(dp, (seq + N_SEQ - 1) % N_SEQ), device_id_type=MESH)

    def ghalo_right():
        return pltpu.make_async_remote_copy(
            grad_right, grad_prev, ghalo_ssem.at[1], ghalo_rsem.at[1],
            device_id=(dp, (seq + 1) % N_SEQ), device_id_type=MESH)

    @pl.when(seq > 0)
    def _():
        ghalo_left().start()

    @pl.when(seq < N_SEQ - 1)
    def _():
        ghalo_right().start()

    shifted = pltpu.roll(g_odd, 1, 0)
    po[pl.ds(0, COARSE)] = (shifted + g_even).astype(BF16)

    @pl.when(seq < N_SEQ - 1)
    def _():
        ghalo_left().wait_recv()

    @pl.when(seq > 0)
    def _():
        ghalo_right().wait_recv()

    grow = iota((16, C_OUT), 0)
    after = grad_next[...].astype(F32)
    prior = grad_prev[...].astype(F32)
    pe[pl.ds(COARSE, 16)] = jnp.where(
        grow == 0, after[:16], jnp.where(grow == 15, prior[:16], 0.0)
    ).astype(BF16)
    prior_odd = pltpu.roll(prior[16:], 1, 0)
    po[pl.ds(0, 16)] = (
        jnp.where(grow == 0, prior_odd, shifted[:16]) + g_even[:16]
    ).astype(BF16)
    last_odd = pltpu.roll(g_odd[COARSE - 16:], 1, 0)
    po[pl.ds(COARSE, 16)] = jnp.where(grow == 0, last_odd + after[16:], 0.0).astype(BF16)

    def out_copy(n):
        cols = pl.ds(pl.multiple_of(n * TILE, TILE), TILE)
        return pltpu.make_async_copy(out_v.at[:, cols], coarse_out.at[0, :, cols], out_sem.at[n])

    def back_tile(n, carry):
        cols = pl.ds(pl.multiple_of(n * TILE, TILE), TILE)
        pairs, cross = pe[...], po[...]
        ahead = dot_nt(pairs, w[0, cols, :]) + dot_nt(cross, w[1, cols, :])
        here = dot_nt(pairs[:COARSE], w[2, cols, :]) + dot_nt(cross[:COARSE], w[3, cols, :])
        behind = dot_nt(pairs, w[4, cols, :])
        total = here + pltpu.roll(ahead, EXT - 1, 0)[:COARSE] + pltpu.roll(behind, 1, 0)[:COARSE]
        out_v[:, cols] = total.astype(BF16)
        out_copy(n).start()
        return carry

    lax.fori_loop(0, C_IN // TILE, back_tile, 0)

    sources = 8

    def second_device(r):
        if_donor = x * 4 + (r // 2) * 2
        if_acceptor = r * 4 + yh * 2 + 1
        return (
            jnp.where(core == 0, if_donor, if_acceptor),
            jnp.where(core == 0, z * 2 + r % 2, seq),
        )

    def chunk_copy(r, source):
        return pltpu.make_async_remote_copy(
            sum1.at[:, r % 2, :, pl.ds((r // 2) * 128, 128)], part2.at[source],
            s2_ssem.at[r], s2_rsem.at[source], device_id=second_device(r), device_id_type=MESH)

    def z_device(zt):
        return (dp, zt * 2 + yl)

    def z_copy(i):
        zt = (z + i) % N_Z
        return pltpu.make_async_remote_copy(
            sum2.at[zt], part3.at[z], s3_ssem.at[i], s3_rsem.at[z],
            device_id=z_device(zt), device_id_type=MESH)

    tile_at = first * 2 + second // 2
    seq_to = z * 2 + second % 2

    def gather_copy(d):
        return pltpu.make_async_remote_copy(
            piece, pieces.at[core, tile_at], ag_ssem.at[d], ag_rsem.at[core, tile_at],
            device_id=(d, seq_to), device_id_type=MESH)

    @pl.when(active)
    def _():
        for s in range(sources):
            @pl.when(s != first * 2 + core)
            def _(s=s):
                for kind in range(2):
                    @pl.when(core == kind)
                    def _(kind=kind):
                        for copy in factor_copies(kind, 0, s):
                            copy.wait_recv()

        for m in range(C_OUT // TILE):
            left = f_act[:, :, m * TILE:(m + 1) * TILE].reshape(sources * SLOTS, TILE)
            right = f_grad[...].reshape(sources * SLOTS, BLOCK)
            block = dot_tn(left, right).astype(BF16)
            for g in range(TILE // 16):
                row = m * TILE + g * 16
                s, at_row = row // ROWS_SEQ, row % ROWS_SEQ
                sum1[s // 2, s % 2, at_row:at_row + 16, :] = block[g * 16:(g + 1) * 16]
        for r in range(4):
            @pl.when(r != second)
            def _(r=r):
                chunk_copy(r, second).start()

            @pl.when(r == second)
            def _(r=r):
                part2[r] = sum1[:, r % 2, :, (r // 2) * 128:(r // 2) * 128 + 128]

        for r in range(4):
            @pl.when(r != second)
            def _(r=r):
                chunk_copy(r, r).wait_recv()

        sum2[...] = (
            part2[0].astype(F32) + part2[1].astype(F32) + part2[2].astype(F32) + part2[3].astype(F32)
        ).astype(BF16)

        for i in range(1, N_Z):
            z_copy(i).start()
        part3[z] = sum2[z]
        for i in range(1, N_Z):
            src = (z + i) % N_Z
            pltpu.make_async_remote_copy(
                sum2.at[src], part3.at[src], s3_ssem.at[i], s3_rsem.at[src],
                device_id=z_device(src), device_id_type=MESH).wait_recv()
        total = part3[0].astype(F32)
        for i in range(1, N_Z):
            total = total + part3[i].astype(F32)
        piece[...] = (total * (1.0 / N_DP)).astype(BF16)

        for d in range(N_DP):
            mine = (d == dp) & (seq_to == seq)

            @pl.when(jnp.logical_not(mine))
            def _(d=d):
                gather_copy(d).start()

            @pl.when(mine)
            def _(d=d):
                pieces[core, tile_at] = piece[...]

    for kind, out in ((0, donor_out), (1, acceptor_out)):
        for t in range(6):
            if kind == 0:
                source = ((t // 2) * 4 + (t % 2) * 2, seq)
            else:
                y_s = t // 2
                source = (((t % 2) * 2 + yl) * 4 + (y_s // 2) * 2 + 1, z * 2 + y_s % 2)
            mine = (source[0] == dp) & (source[1] == seq)

            @pl.when(jnp.logical_not(mine))
            def _(kind=kind, t=t, source=source):
                pltpu.make_async_remote_copy(
                    piece, pieces.at[kind, t], ag_ssem.at[0], ag_rsem.at[kind, t],
                    device_id=source, device_id_type=MESH).wait_recv()

            out[:, t * 128:(t + 1) * 128] = pieces[kind, t].astype(F32)

    lax.fori_loop(0, C_IN // TILE, lambda n, carry: (out_copy(n).wait(), carry)[1], 0)

    @pl.when(seq > 0)
    def _():
        halo_left().wait_send()
        ghalo_left().wait_send()

    @pl.when(seq < N_SEQ - 1)
    def _():
        halo_right().wait_send()
        ghalo_right().wait_send()

    lax.fori_loop(1, N_SEQ, lambda i, carry: (pos_copy(i).wait_send(), carry)[1], 0)
    a1_drain()
    a2_drain()
    for kind in range(2):
        for p in range(3):
            mine = (core == kind) & (ring_at[kind] == p)

            @pl.when(jnp.logical_not(mine))
            def _(kind=kind, p=p):
                for copy in factor_copies(kind, p, 0):
                    copy.wait_send()

    @pl.when(active)
    def _():
        for r in range(4):
            @pl.when(r != second)
            def _(r=r):
                chunk_copy(r, second).wait_send()
        for i in range(1, N_Z):
            z_copy(i).wait_send()
        for d in range(N_DP):
            @pl.when(jnp.logical_not((d == dp) & (seq_to == seq)))
            def _(d=d):
                gather_copy(d).wait_send()


def on_device(*args):
    vmem = pl.BlockSpec(memory_space=pltpu.VMEM)
    hbm = pl.BlockSpec(memory_space=pl.ANY)
    dma = pltpu.SemaphoreType.DMA

    def v(*shape, dtype=BF16):
        return pltpu.VMEM(shape, dtype)

    scratch = [
        v(TAPS, C_IN, C_OUT), v(C_OUT, EMB), v(C_OUT, EMB), v(EXT, C_IN),
        v(FINE, C_OUT), v(FINE, C_OUT), v(FINE, C_OUT), v(FINE, C_OUT),
        v(FINE, C_OUT), v(FINE, C_OUT, dtype=F32),
        v(16, C_IN), v(16, C_IN), v(32, C_OUT), v(32, C_OUT), v(32, C_OUT), v(32, C_OUT),
        v(8, 128, dtype=I32), v(N_SEQ, 8, 128, dtype=I32),
        v(N_SEQ, 16, HALF), v(N_SEQ, 16, HALF), v(N_SEQ, 16, HALF), v(N_SEQ, 16, HALF),
        v(EXT, C_OUT), v(EXT, C_OUT), v(COARSE, C_IN),
        v(SLOTS, C_OUT), v(SLOTS, EMB), v(SLOTS, C_OUT), v(SLOTS, EMB),
        v(8, SLOTS, C_OUT), v(8, SLOTS, BLOCK), v(N_Z, 2, ROWS_SEQ, BLOCK),
        v(4, N_Z, ROWS_SEQ, 128), v(N_Z, ROWS_SEQ, 128), v(N_Z, ROWS_SEQ, 128),
        v(ROWS_SEQ, 128), v(2, 6, ROWS_SEQ, 128),
        dma((5,)), dma((3,)), dma((4,)), dma((2,)), dma((2,)), dma((2,)), dma((2,)),
        dma((N_SEQ,)), dma((N_SEQ,)), dma((N_SEQ,)), dma((N_SEQ,)), dma((N_SEQ,)), dma((N_SEQ,)),
        dma((6,)), dma((8,)), dma((6,)), dma((8,)), dma((2,)),
        dma((4,)), dma((4,)), dma((N_Z,)), dma((N_Z,)), dma((N_DP,)), dma((2, 6)),
    ]
    return pl.pallas_call(
        kernel,
        out_shape=(
            jax.ShapeDtypeStruct((1, SLOTS), F32),
            jax.ShapeDtypeStruct((1, COARSE, C_IN), BF16),
            jax.ShapeDtypeStruct((ROWS_SEQ, EMB), F32),
            jax.ShapeDtypeStruct((ROWS_SEQ, EMB), F32),
        ),
        in_specs=[hbm] * 6 + [vmem] * 4,
        out_specs=(vmem, hbm, vmem, vmem),
        scratch_shapes=scratch,
        compiler_params=pltpu.CompilerParams(
            collective_id=0, has_side_effects=True, vmem_limit_bytes=48 * 1024 * 1024
        ),
    )(*args)


def solution(mesh):
    rows, slots = P("dp", "seq", None), P("dp", "seq")
    return jax.shard_map(
        on_device,
        mesh=mesh,
        in_specs=(rows, rows, P(), P(), P(), rows, slots, slots, slots, slots),
        out_specs=(slots, rows, P("seq", None), P("seq", None)),
        check_vma=False,
    )
```

```python
import math

import jax
import jax.numpy as jnp
from jax import lax
from jax.experimental import pallas as pl
from jax.experimental.pallas import tpu as pltpu
from jax.sharding import PartitionSpec as P

MESH = pl.DeviceIdType.MESH
F32, BF16, I32 = jnp.float32, jnp.bfloat16, jnp.int32
N_X, N_Y, N_Z = 4, 4, 8
N_DP, N_SEQ = 16, 16
COARSE, FINE, C_IN, C_OUT, EMB = 256, 512, 1024, 768, 768
EXT = COARSE + 16
TAPS, ACAP, SLOTS = 5, 8, 64
CAP = N_SEQ * ACAP
TILE = 256
HALF = 384
BLOCK = 256
ROWS_SEQ = C_OUT // N_SEQ
INV_ROOT = 1.0 / math.sqrt(EMB)
K0 = math.sqrt(2.0 / math.pi)
K1 = 0.044715


def dot(a, b):
    return jnp.dot(a, b, preferred_element_type=F32)


def dot_nt(a, b):
    return lax.dot_general(a, b, (((1,), (1,)), ((), ())), preferred_element_type=F32)


def dot_tn(a, b):
    return lax.dot_general(a, b, (((0,), (0,)), ((), ())), preferred_element_type=F32)


def one_hot(condition):
    return jnp.where(condition, 1.0, 0.0).astype(BF16)


def iota(shape, axis):
    return lax.broadcasted_iota(I32, shape, axis)


def as_column(row):
    return jnp.transpose(jnp.broadcast_to(row, (128, 128)))[:, 0:1]


def as_row(column):
    return jnp.transpose(jnp.broadcast_to(column, (128, 128)))[0:1, :]


def folded(row):
    return jnp.where(row < 0, -1, (row & 1) * COARSE + (row >> 1))


def pack(rows):
    cells = rows.reshape(N_SEQ, ACAP, EMB)
    return jnp.concatenate([cells[:, :, :HALF], cells[:, :, HALF:]], axis=1).astype(BF16)


def unpack(cells):
    wide = cells.astype(F32)
    both = jnp.concatenate([wide[:, :ACAP], wide[:, ACAP:]], axis=2)
    return both.reshape(CAP, EMB).astype(BF16)


def kernel(
    coarse, skip, conv_w, donor_w, acceptor_w, other, score_grad, donor_pos, acceptor_pos, mask,
    scores_out, coarse_out, donor_out, acceptor_out,
    score_v, donor_v, acceptor_v, mask_v, w, wd, wa, c_ext, skip_in, other_in, skip_f, other_f, act, slope,
    halo_next, halo_prev, grad_next, grad_prev, grad_left, grad_right,
    pos_own, pos_all, a1_send, a1_recv, a2_send, a2_recv,
    pe, po, dact, dgrad, aact, agrad,
    f_act, f_grad, sum1, part2, sum2, part3, piece, pieces,
    load_sem, w_sem, halo_ssem, halo_rsem, ghalo_ssem, ghalo_rsem,
    pos_ssem, pos_rsem, a1_ssem, a1_rsem, a2_ssem, a2_rsem,
    f_ssem, f_rsem, g_ssem, g_rsem,
    s2_ssem, s2_rsem, s3_ssem, s3_rsem, ag_ssem, ag_rsem,
):
    dp, seq = lax.axis_index("dp"), lax.axis_index("seq")
    x, yh, core = dp // 4, (dp // 2) % 2, dp % 2
    z, yl = seq // 2, seq % 2
    y = yh * 2 + yl

    drains = []

    def finish():
        for drain in drains:
            drain()

    def when(condition, action):
        pl.when(condition)(action)

    smalls = (score_grad, donor_pos, acceptor_pos, mask)
    held = (score_v, donor_v, acceptor_v, mask_v)
    small_loads = [
        pltpu.make_async_copy(a, b, load_sem.at[5 + i]) for i, (a, b) in enumerate(zip(smalls, held))
    ]
    loads = [
        pltpu.make_async_copy(coarse.at[0], c_ext.at[pl.ds(0, COARSE)], load_sem.at[0]),
        pltpu.make_async_copy(skip.at[0], skip_in, load_sem.at[1]),
        pltpu.make_async_copy(donor_w, wd, load_sem.at[2]),
        pltpu.make_async_copy(acceptor_w, wa, load_sem.at[3]),
        pltpu.make_async_copy(other.at[0], other_in, load_sem.at[4]),
    ]

    def load_w(n):
        cols = pl.ds(pl.multiple_of(n * TILE, TILE), TILE)
        return pltpu.make_async_copy(conv_w.at[:, :, cols], w.at[:, :, cols], w_sem.at[n])

    for load in small_loads:
        load.start()
    loads[0].start()

    halo_next[...] = jnp.zeros_like(halo_next)
    halo_prev[...] = jnp.zeros_like(halo_prev)
    grad_next[...] = jnp.zeros_like(grad_next)
    grad_prev[...] = jnp.zeros_like(grad_prev)
    barrier = pltpu.get_barrier_semaphore()

    def greet_seq(i, carry):
        pl.semaphore_signal(barrier, inc=1, device_id=(dp, (seq + i) % N_SEQ), device_id_type=MESH)
        return carry

    def greet_dp(i, carry):
        other_dp = (dp + i) % N_DP
        pl.semaphore_signal(barrier, inc=1, device_id=(other_dp, seq), device_id_type=MESH)
        pl.semaphore_signal(
            barrier, inc=1, device_id=(other_dp, z * 2 + 1 - yl), device_id_type=MESH
        )
        return carry

    lax.fori_loop(1, N_SEQ, greet_seq, 0)
    lax.fori_loop(1, N_DP, greet_dp, 0)
    load_w(0).start()
    loads[1].start()
    for n in range(1, C_OUT // TILE):
        load_w(n).start()
    for load in loads[2:]:
        load.start()
    for load in small_loads:
        load.wait()
    own_row = jnp.concatenate([acceptor_v[...], jnp.full((1, 64), -1, I32)], axis=1)
    pos_own[...] = jnp.broadcast_to(own_row, (8, 128))
    loads[0].wait()
    pl.semaphore_wait(barrier, N_SEQ - 1 + 2 * (N_DP - 1))


    def halo_left():
        return pltpu.make_async_remote_copy(
            c_ext.at[pl.ds(0, 16)], halo_next, halo_ssem.at[0], halo_rsem.at[0],
            device_id=(dp, (seq + N_SEQ - 1) % N_SEQ), device_id_type=MESH)

    def halo_right():
        return pltpu.make_async_remote_copy(
            c_ext.at[pl.ds(COARSE - 16, 16)], halo_prev, halo_ssem.at[1], halo_rsem.at[1],
            device_id=(dp, (seq + 1) % N_SEQ), device_id_type=MESH)

    when(seq > 0, lambda: halo_left().start())
    when(seq < N_SEQ - 1, lambda: halo_right().start())
    drains.append(lambda: when(seq > 0, lambda: halo_left().wait_send()))
    drains.append(lambda: when(seq < N_SEQ - 1, lambda: halo_right().wait_send()))

    def pos_copy(i):
        return pltpu.make_async_remote_copy(
            pos_own, pos_all.at[seq], pos_ssem.at[i], pos_rsem.at[seq],
            device_id=(dp, (seq + i) % N_SEQ), device_id_type=MESH)

    def pos_start(i, carry):
        pos_copy(i).start()
        return carry

    lax.fori_loop(1, N_SEQ, pos_start, 0)
    drains.append(
        lambda: lax.fori_loop(1, N_SEQ, lambda i, carry: (pos_copy(i).wait_send(), carry)[1], 0)
    )
    pos_all[seq] = pos_own[...]

    loads[1].wait()
    at = iota((COARSE, FINE), 1)
    step2 = 2 * iota((COARSE, FINE), 0)
    even, odd = one_hot(at == step2), one_hot(at == step2 + 1)
    skip_f[pl.ds(0, COARSE)] = dot(even, skip_in[...]).astype(BF16)
    skip_f[pl.ds(COARSE, COARSE)] = dot(odd, skip_in[...]).astype(BF16)

    sub, lane = iota((128, 128), 0), iota((128, 128), 1)
    before = one_hot(sub < lane)
    place = sub % ACAP
    own = jnp.broadcast_to(own_row, (128, 128))
    own_hit = (own >> 9) == sub // ACAP
    own_rank = dot(one_hot(own_hit), before).astype(I32)
    to_served = jnp.where(own_hit & (own_rank == place), 1.0, 0.0)
    from_served = jnp.transpose(to_served)[:SLOTS].astype(BF16)
    to_served = to_served[:, :SLOTS].astype(BF16)
    pad = jnp.full((1, 64), -1, I32)
    donor_row = folded(jnp.concatenate([donor_v[...], pad], axis=1))
    donor_column = as_column(donor_row.astype(F32)).astype(I32)[:SLOTS]
    from_donor = one_hot(iota((SLOTS, FINE), 1) == donor_column)
    to_donor = one_hot(iota((FINE, 128), 0) == donor_row)
    fpad = jnp.zeros((1, 64), F32)
    mask_column = as_column(jnp.concatenate([mask_v[...].astype(F32), fpad], axis=1))[:SLOTS]
    score_column = as_column(jnp.concatenate([score_v[...], fpad], axis=1))[:SLOTS]
    weighted = score_column * mask_column

    when(seq < N_SEQ - 1, lambda: halo_left().wait_recv())
    when(seq > 0, lambda: halo_right().wait_recv())

    row16 = iota((16, C_IN), 0)
    c_ext[pl.ds(COARSE, 16)] = jnp.where(
        row16 == 0, halo_next[...].astype(F32),
        jnp.where(row16 == 15, halo_prev[...].astype(F32), 0.0),
    ).astype(BF16)

    def conv_tile(n, carry):
        load_w(n).wait()
        cols = pl.ds(pl.multiple_of(n * TILE, TILE), TILE)
        cells = c_ext[...]
        taps = [dot(cells, w[k, :, cols]) for k in range(TAPS)]
        even_sum = (
            pltpu.roll(taps[0] + taps[1], 1, 0) + taps[2] + taps[3] + pltpu.roll(taps[4], EXT - 1, 0)
        )
        odd_sum = (
            pltpu.roll(taps[0], 1, 0) + taps[1] + taps[2] + pltpu.roll(taps[3] + taps[4], EXT - 1, 0)
        )
        for part, total in ((0, even_sum), (1, odd_sum)):
            rows = pl.ds(part * COARSE, COARSE)
            v = total[:COARSE] + skip_f[rows, cols].astype(F32)
            square = v * v
            t = jnp.tanh(K0 * v * (1.0 + K1 * square))
            half = 0.5 * (1.0 + t)
            act[rows, cols] = (v * half).astype(BF16)
            slope[rows, cols] = half + 0.5 * v * (1.0 - t * t) * (K0 * (1.0 + 3.0 * K1 * square))
        return carry

    lax.fori_loop(0, C_OUT // TILE, conv_tile, 0)

    def pos_wait(i, carry):
        src = (seq + i) % N_SEQ
        pltpu.make_async_remote_copy(
            pos_own, pos_all.at[src], pos_ssem.at[i], pos_rsem.at[src],
            device_id=(dp, src), device_id_type=MESH).wait_recv()
        return carry

    lax.fori_loop(1, N_SEQ, pos_wait, 0)
    named = pos_all[...].reshape(CAP, 128)
    hit = (named >> 9) == seq
    rank = dot(one_hot(hit), before).astype(I32)
    chosen = jnp.where(hit & (rank == place), (named & (FINE - 1)) + 1, 0).astype(F32)
    served = jnp.sum(chosen, axis=1, keepdims=True).astype(I32) - 1
    served = folded(served)
    from_rows = one_hot(iota((CAP, FINE), 1) == served)
    served_row = as_row(served.astype(F32)).astype(I32)
    to_rows = one_hot(iota((FINE, CAP), 0) == served_row)
    a1_send[...] = pack(dot(from_rows, act[...]))

    def exchange(send, recv, ssem, rsem):
        def copy(i):
            peer = (seq + i) % N_SEQ
            return pltpu.make_async_remote_copy(
                send.at[peer], recv.at[seq], ssem.at[i], rsem.at[seq],
                device_id=(dp, peer), device_id_type=MESH)

        def start(i, carry):
            copy(i).start()
            return carry

        def wait(i, carry):
            src = (seq + i) % N_SEQ
            pltpu.make_async_remote_copy(
                send.at[src], recv.at[src], ssem.at[i], rsem.at[src],
                device_id=(dp, src), device_id_type=MESH).wait_recv()
            return carry

        def drain(i, carry):
            copy(i).wait_send()
            return carry

        return [lambda f=f: lax.fori_loop(1, N_SEQ, f, 0) for f in (start, wait, drain)]

    a1_start, a1_wait, a1_drain = exchange(a1_send, a1_recv, a1_ssem, a1_rsem)
    a2_start, a2_wait, a2_drain = exchange(a2_send, a2_recv, a2_ssem, a2_rsem)
    a1_start()
    drains.append(a1_drain)
    a1_recv[seq] = a1_send[seq]

    acts, grads = (dact, aact), (dgrad, agrad)
    ring_at = (x, y)
    first = jnp.where(core == 0, x, y)
    second = jnp.where(core == 0, y, x)
    active = first < 3

    def target(kind, p):
        if kind == 0:
            return (p * 4 + yh * 2, seq)
        return (x * 4 + (p // 2) * 2 + 1, z * 2 + p % 2)

    def act_copy(kind, p, source):
        return pltpu.make_async_remote_copy(
            acts[kind], f_act.at[source], f_ssem.at[kind * 3 + p], f_rsem.at[source],
            device_id=target(kind, p), device_id_type=MESH)

    def grad_copy(kind, p, source):
        return pltpu.make_async_remote_copy(
            grads[kind].at[:, pl.ds(p * BLOCK, BLOCK)], f_grad.at[source],
            g_ssem.at[kind * 3 + p], g_rsem.at[source],
            device_id=target(kind, p), device_id_type=MESH)

    def give_factor(kind, copy_of, keep):
        source = ring_at[kind] * 2 + core
        for p in range(3):
            mine = (core == kind) & (ring_at[kind] == p)
            when(jnp.logical_not(mine), lambda: copy_of(kind, p, source).start())
            when(mine, lambda: keep(source, p))
            drains.append(
                lambda p=p, mine=mine: when(
                    jnp.logical_not(mine), lambda: copy_of(kind, p, 0).wait_send()
                )
            )

    def give_act(kind):
        def keep(source, p):
            f_act[source] = acts[kind][...]

        give_factor(kind, act_copy, keep)

    def give_grad(kind):
        def keep(source, p):
            f_grad[source] = grads[kind][:, p * BLOCK:(p + 1) * BLOCK]

        give_factor(kind, grad_copy, keep)

    loads[2].wait()
    loads[3].wait()
    donor_act = dot(from_donor, act[...]).astype(BF16)
    donor_emb = dot(donor_act, wd[...]).astype(BF16).astype(F32)
    acceptor_emb_grad = (weighted * donor_emb * INV_ROOT).astype(BF16)
    acceptor_rows = dot_nt(acceptor_emb_grad, wa[...]).astype(BF16)
    a2_send[...] = pack(dot(to_served, acceptor_rows))
    dact[...] = donor_act
    agrad[...] = acceptor_emb_grad
    a2_start()
    give_act(0)
    give_grad(1)
    drains.append(a2_drain)
    a2_recv[seq] = a2_send[seq]

    loads[4].wait()
    other_f[pl.ds(0, COARSE)] = dot(even, other_in[...]).astype(BF16)
    other_f[pl.ds(COARSE, COARSE)] = dot(odd, other_in[...]).astype(BF16)

    a1_wait()
    acceptor_act = dot(from_served, unpack(a1_recv[...])).astype(BF16)
    acceptor_emb = dot(acceptor_act, wa[...]).astype(BF16).astype(F32)
    score = mask_column * jnp.sum(donor_emb * acceptor_emb, axis=1, keepdims=True) * INV_ROOT
    score = jnp.concatenate([score, jnp.zeros((128 - SLOTS, 1), F32)], axis=0)
    scores_out[...] = as_row(score)[:, :SLOTS]
    donor_emb_grad = (weighted * acceptor_emb * INV_ROOT).astype(BF16)
    aact[...] = acceptor_act
    dgrad[...] = donor_emb_grad

    give_grad(0)
    give_act(1)

    sources = 8

    def second_device(r):
        if_donor = x * 4 + (r // 2) * 2
        if_acceptor = r * 4 + yh * 2 + 1
        return (
            jnp.where(core == 0, if_donor, if_acceptor),
            jnp.where(core == 0, z * 2 + r % 2, seq),
        )

    def chunk_copy(r, source):
        return pltpu.make_async_remote_copy(
            sum1.at[:, r % 2, :, pl.ds((r // 2) * 128, 128)], part2.at[source],
            s2_ssem.at[r], s2_rsem.at[source], device_id=second_device(r), device_id_type=MESH)

    def z_device(zt):
        return (dp, zt * 2 + yl)

    def z_copy(i):
        zt = (z + i) % N_Z
        return pltpu.make_async_remote_copy(
            sum2.at[zt], part3.at[z], s3_ssem.at[i], s3_rsem.at[z],
            device_id=z_device(zt), device_id_type=MESH)

    tile_at = first * 2 + second // 2
    seq_to = z * 2 + second % 2

    def gather_copy(d):
        return pltpu.make_async_remote_copy(
            piece, pieces.at[core, tile_at], ag_ssem.at[d], ag_rsem.at[core, tile_at],
            device_id=(d, seq_to), device_id_type=MESH)

    def block_sum():
        for s in range(sources):
            @pl.when(s != first * 2 + core)
            def _(s=s):
                for kind in range(2):
                    @pl.when(core == kind)
                    def _(kind=kind):
                        act_copy(kind, 0, s).wait_recv()
                        grad_copy(kind, 0, s).wait_recv()

        for m in range(C_OUT // TILE):
            left = f_act[:, :, m * TILE:(m + 1) * TILE].reshape(sources * SLOTS, TILE)
            right = f_grad[...].reshape(sources * SLOTS, BLOCK)
            block = dot_tn(left, right).astype(BF16)
            for g in range(TILE // 16):
                row = m * TILE + g * 16
                s, at_row = row // ROWS_SEQ, row % ROWS_SEQ
                sum1[s // 2, s % 2, at_row:at_row + 16, :] = block[g * 16:(g + 1) * 16]
        for r in range(4):
            when(r != second, lambda: chunk_copy(r, second).start())

            @pl.when(r == second)
            def _(r=r):
                part2[r] = sum1[:, r % 2, :, (r // 2) * 128:(r // 2) * 128 + 128]

    def block_drain():
        for r in range(4):
            when(r != second, lambda: chunk_copy(r, second).wait_send())

    def ring_sum():
        for r in range(4):
            when(r != second, lambda: chunk_copy(r, r).wait_recv())
        sum2[...] = (
            part2[0].astype(F32) + part2[1].astype(F32) + part2[2].astype(F32) + part2[3].astype(F32)
        ).astype(BF16)
        for i in range(1, N_Z):
            z_copy(i).start()
        part3[z] = sum2[z]

    def ring_drain():
        for i in range(1, N_Z):
            z_copy(i).wait_send()

    def z_sum():
        for i in range(1, N_Z):
            src = (z + i) % N_Z
            pltpu.make_async_remote_copy(
                sum2.at[src], part3.at[src], s3_ssem.at[i], s3_rsem.at[src],
                device_id=z_device(src), device_id_type=MESH).wait_recv()
        total = part3[0].astype(F32)
        for i in range(1, N_Z):
            total = total + part3[i].astype(F32)
        piece[...] = (total * (1.0 / N_DP)).astype(BF16)
        for d in range(N_DP):
            mine = (d == dp) & (seq_to == seq)
            when(jnp.logical_not(mine), lambda: gather_copy(d).start())

            @pl.when(mine)
            def _(d=d):
                pieces[core, tile_at] = piece[...]

    def z_drain():
        for d in range(N_DP):
            when(jnp.logical_not((d == dp) & (seq_to == seq)), lambda: gather_copy(d).wait_send())

    donor_rows = dot_nt(donor_emb_grad, wd[...]).astype(BF16)
    a2_wait()
    served_rows = unpack(a2_recv[...])

    def grad_of(rows):
        total = (
            other_f[rows].astype(F32)
            + dot(to_rows[rows.start:rows.start + rows.size], served_rows)
            + dot(to_donor[rows.start:rows.start + rows.size, :SLOTS], donor_rows)
        )
        return total * slope[rows]

    g_even = grad_of(pl.ds(0, COARSE))
    g_odd = grad_of(pl.ds(COARSE, COARSE))
    pair = g_even + g_odd
    pe[pl.ds(0, COARSE)] = pair.astype(BF16)
    grad_left[pl.ds(0, 16)] = pair[:16].astype(BF16)
    grad_left[pl.ds(16, 16)] = g_even[:16].astype(BF16)
    grad_right[pl.ds(0, 16)] = pair[COARSE - 16:].astype(BF16)
    grad_right[pl.ds(16, 16)] = g_odd[COARSE - 16:].astype(BF16)

    def ghalo_left():
        return pltpu.make_async_remote_copy(
            grad_left, grad_next, ghalo_ssem.at[0], ghalo_rsem.at[0],
            device_id=(dp, (seq + N_SEQ - 1) % N_SEQ), device_id_type=MESH)

    def ghalo_right():
        return pltpu.make_async_remote_copy(
            grad_right, grad_prev, ghalo_ssem.at[1], ghalo_rsem.at[1],
            device_id=(dp, (seq + 1) % N_SEQ), device_id_type=MESH)

    when(seq > 0, lambda: ghalo_left().start())
    when(seq < N_SEQ - 1, lambda: ghalo_right().start())
    drains.append(lambda: when(seq > 0, lambda: ghalo_left().wait_send()))
    drains.append(lambda: when(seq < N_SEQ - 1, lambda: ghalo_right().wait_send()))

    shifted = pltpu.roll(g_odd, 1, 0)
    po[pl.ds(0, COARSE)] = (shifted + g_even).astype(BF16)

    when(active, block_sum)
    drains.append(lambda: when(active, block_drain))

    when(seq < N_SEQ - 1, lambda: ghalo_left().wait_recv())
    when(seq > 0, lambda: ghalo_right().wait_recv())

    grow = iota((16, C_OUT), 0)
    after = grad_next[...].astype(F32)
    prior = grad_prev[...].astype(F32)
    pe[pl.ds(COARSE, 16)] = jnp.where(
        grow == 0, after[:16], jnp.where(grow == 15, prior[:16], 0.0)
    ).astype(BF16)
    prior_odd = pltpu.roll(prior[16:], 1, 0)
    po[pl.ds(0, 16)] = (
        jnp.where(grow == 0, prior_odd, shifted[:16]) + g_even[:16]
    ).astype(BF16)
    last_odd = pltpu.roll(g_odd[COARSE - 16:], 1, 0)
    po[pl.ds(COARSE, 16)] = jnp.where(grow == 0, last_odd + after[16:], 0.0).astype(BF16)

    def back_tile(n, carry):
        cols = pl.ds(pl.multiple_of(n * TILE, TILE), TILE)
        pairs, cross = pe[...], po[...]
        ahead = dot_nt(pairs, w[0, cols, :]) + dot_nt(cross, w[1, cols, :])
        here = dot_nt(pairs[:COARSE], w[2, cols, :]) + dot_nt(cross[:COARSE], w[3, cols, :])
        behind = dot_nt(pairs, w[4, cols, :])
        total = here + pltpu.roll(ahead, EXT - 1, 0)[:COARSE] + pltpu.roll(behind, 1, 0)[:COARSE]
        coarse_out[0, :, cols] = total.astype(BF16)
        return carry

    lax.fori_loop(0, C_IN // TILE, back_tile, 0)
    when(active, ring_sum)
    drains.append(lambda: when(active, ring_drain))

    when(active, z_sum)
    drains.append(lambda: when(active, z_drain))

    for kind, out in ((0, donor_out), (1, acceptor_out)):
        for t in range(6):
            if kind == 0:
                source = ((t // 2) * 4 + (t % 2) * 2, seq)
            else:
                y_s = t // 2
                source = (((t % 2) * 2 + yl) * 4 + (y_s // 2) * 2 + 1, z * 2 + y_s % 2)
            mine = (source[0] == dp) & (source[1] == seq)

            @pl.when(jnp.logical_not(mine))
            def _(kind=kind, t=t, source=source):
                pltpu.make_async_remote_copy(
                    piece, pieces.at[kind, t], ag_ssem.at[0], ag_rsem.at[kind, t],
                    device_id=source, device_id_type=MESH).wait_recv()

            out[:, t * 128:(t + 1) * 128] = pieces[kind, t].astype(F32)

    finish()


def write_out(*refs):
    sem = refs[8]
    copies = [pltpu.make_async_copy(refs[i], refs[4 + i], sem.at[i]) for i in range(4)]
    for copy in copies:
        copy.start()
    for copy in copies:
        copy.wait()


def on_device(*args):
    vmem = pl.BlockSpec(memory_space=pltpu.VMEM)
    hbm = pl.BlockSpec(memory_space=pltpu.HBM)
    dma = pltpu.SemaphoreType.DMA

    def v(*shape, dtype=BF16):
        return pltpu.VMEM(shape, dtype)

    scratch = [
        v(1, SLOTS, dtype=F32), v(1, SLOTS, dtype=I32), v(1, SLOTS, dtype=I32), v(1, SLOTS, dtype=I32),
        v(TAPS, C_IN, C_OUT), v(C_OUT, EMB), v(C_OUT, EMB), v(EXT, C_IN),
        v(FINE, C_OUT), v(FINE, C_OUT), v(FINE, C_OUT), v(FINE, C_OUT),
        v(FINE, C_OUT), v(FINE, C_OUT, dtype=F32),
        v(16, C_IN), v(16, C_IN), v(32, C_OUT), v(32, C_OUT), v(32, C_OUT), v(32, C_OUT),
        v(8, 128, dtype=I32), v(N_SEQ, 8, 128, dtype=I32),
        v(N_SEQ, 16, HALF), v(N_SEQ, 16, HALF), v(N_SEQ, 16, HALF), v(N_SEQ, 16, HALF),
        v(EXT, C_OUT), v(EXT, C_OUT),
        v(SLOTS, C_OUT), v(SLOTS, EMB), v(SLOTS, C_OUT), v(SLOTS, EMB),
        v(8, SLOTS, C_OUT), v(8, SLOTS, BLOCK), v(N_Z, 2, ROWS_SEQ, BLOCK),
        v(4, N_Z, ROWS_SEQ, 128), v(N_Z, ROWS_SEQ, 128), v(N_Z, ROWS_SEQ, 128),
        v(ROWS_SEQ, 128), v(2, 6, ROWS_SEQ, 128),
        dma((9,)), dma((3,)), dma((2,)), dma((2,)), dma((2,)), dma((2,)),
        dma((N_SEQ,)), dma((N_SEQ,)), dma((N_SEQ,)), dma((N_SEQ,)), dma((N_SEQ,)), dma((N_SEQ,)),
        dma((6,)), dma((8,)), dma((6,)), dma((8,)),
        dma((4,)), dma((4,)), dma((N_Z,)), dma((N_Z,)), dma((N_DP,)), dma((2, 6)),
    ]
    shapes = (
        jax.ShapeDtypeStruct((1, SLOTS), F32),
        jax.ShapeDtypeStruct((1, COARSE, C_IN), BF16),
        jax.ShapeDtypeStruct((ROWS_SEQ, EMB), F32),
        jax.ShapeDtypeStruct((ROWS_SEQ, EMB), F32),
    )
    args = [pltpu.with_memory_space_constraint(a, pltpu.HBM) for a in args]
    results = pl.pallas_call(
        kernel,
        out_shape=shapes,
        in_specs=[hbm] * 10,
        out_specs=(vmem,) * 4,
        scratch_shapes=scratch,
        compiler_params=pltpu.CompilerParams(
            collective_id=0, has_side_effects=True, vmem_limit_bytes=48*1024*1024
        ),
    )(*args)
    return pl.pallas_call(
        write_out,
        out_shape=shapes,
        in_specs=[vmem] * 4,
        out_specs=(pl.BlockSpec(memory_space=pl.ANY),) * 4,
        scratch_shapes=[dma((4,))],
        compiler_params=pltpu.CompilerParams(vmem_limit_bytes=1024 * 1024),
    )(*results)


def solution(mesh):
    rows, slots = P("dp", "seq", None), P("dp", "seq")
    return jax.shard_map(
        on_device,
        mesh=mesh,
        in_specs=(rows, rows, P(), P(), P(), rows, slots, slots, slots, slots),
        out_specs=(slots, rows, P("seq", None), P("seq", None)),
        check_vma=False,
    )
```

```python
import math

import jax
import jax.numpy as jnp
from jax import lax
from jax.experimental import pallas as pl
from jax.experimental.pallas import tpu as pltpu
from jax.sharding import PartitionSpec as P

MESH = pl.DeviceIdType.MESH
F32, BF16, I32 = jnp.float32, jnp.bfloat16, jnp.int32
N_X, N_Y, N_Z = 4, 4, 8
N_DP, N_SEQ = 16, 16
COARSE, FINE, C_IN, C_OUT, EMB = 256, 512, 1024, 768, 768
EXT = COARSE + 16
TAPS, ACAP, SLOTS = 5, 8, 64
CAP = N_SEQ * ACAP
TILE = 256
HALF = 384
BLOCKS = (((1, 2), (0, 0), (0, 1)), ((1, 0), (0, 2), (1, 1)))
BLOCK = 256
ROWS_SEQ = C_OUT // N_SEQ
INV_ROOT = 1.0 / math.sqrt(EMB)
K0 = math.sqrt(2.0 / math.pi)
K1 = 0.044715


def dot(a, b):
    return jnp.dot(a, b, preferred_element_type=F32)


def dot_nt(a, b):
    return lax.dot_general(a, b, (((1,), (1,)), ((), ())), preferred_element_type=F32)


def dot_tn(a, b):
    return lax.dot_general(a, b, (((0,), (0,)), ((), ())), preferred_element_type=F32)


def one_hot(condition):
    return jnp.where(condition, 1.0, 0.0).astype(BF16)


def iota(shape, axis):
    return lax.broadcasted_iota(I32, shape, axis)


def as_column(row):
    return jnp.transpose(jnp.broadcast_to(row, (128, 128)))[:, 0:1]


def as_row(column):
    return jnp.transpose(jnp.broadcast_to(column, (128, 128)))[0:1, :]


def folded(row):
    return jnp.where(row < 0, -1, (row & 1) * COARSE + (row >> 1))


def pack(rows):
    cells = rows.reshape(N_SEQ, ACAP, EMB)
    return jnp.concatenate([cells[:, :, :HALF], cells[:, :, HALF:]], axis=1).astype(BF16)


def unpack(cells):
    wide = cells.astype(F32)
    both = jnp.concatenate([wide[:, :ACAP], wide[:, ACAP:]], axis=2)
    return both.reshape(CAP, EMB).astype(BF16)


def kernel(
    coarse, skip, conv_w, donor_w, acceptor_w, other, score_grad, donor_pos, acceptor_pos, mask,
    scores_out, coarse_out, donor_out, acceptor_out,
    score_v, donor_v, acceptor_v, mask_v, w, wd, wa, c_ext, skip_in, other_in, skip_f, other_f, act, slope,
    halo_next, halo_prev, grad_next, grad_prev, grad_left, grad_right,
    pos_own, pos_all, a1_send, a1_recv, a2_send, a2_recv,
    pe, po, dact, dgrad, aact, agrad,
    f_act, f_grad, sum1, act_t, part2, sum2, part3, piece, pieces,
    load_sem, w_sem, halo_ssem, halo_rsem, ghalo_ssem, ghalo_rsem,
    pos_ssem, pos_rsem, a1_ssem, a1_rsem, a2_ssem, a2_rsem,
    f_ssem, f_rsem, g_ssem, g_rsem,
    s2_ssem, s2_rsem, s3_ssem, s3_rsem, ag_ssem, ag_rsem,
):
    dp, seq = lax.axis_index("dp"), lax.axis_index("seq")
    x, yh, core = dp // 4, (dp // 2) % 2, dp % 2
    z, yl = seq // 2, seq % 2
    y = yh * 2 + yl

    drains = []

    def finish():
        for drain in drains:
            drain()

    def when(condition, action):
        pl.when(condition)(action)

    smalls = (score_grad, donor_pos, acceptor_pos, mask)
    held = (score_v, donor_v, acceptor_v, mask_v)
    small_loads = [
        pltpu.make_async_copy(a, b, load_sem.at[5 + i]) for i, (a, b) in enumerate(zip(smalls, held))
    ]
    loads = [
        pltpu.make_async_copy(coarse.at[0], c_ext.at[pl.ds(0, COARSE)], load_sem.at[0]),
        pltpu.make_async_copy(skip.at[0], skip_in, load_sem.at[1]),
        pltpu.make_async_copy(donor_w, wd, load_sem.at[2]),
        pltpu.make_async_copy(acceptor_w, wa, load_sem.at[3]),
        pltpu.make_async_copy(other.at[0], other_in, load_sem.at[4]),
    ]

    def load_w(n):
        cols = pl.ds(pl.multiple_of(n * TILE, TILE), TILE)
        return pltpu.make_async_copy(conv_w.at[:, :, cols], w.at[:, :, cols], w_sem.at[n])

    for load in small_loads:
        load.start()
    loads[0].start()

    halo_next[...] = jnp.zeros_like(halo_next)
    halo_prev[...] = jnp.zeros_like(halo_prev)
    grad_next[...] = jnp.zeros_like(grad_next)
    grad_prev[...] = jnp.zeros_like(grad_prev)
    barrier = pltpu.get_barrier_semaphore()

    def greet_seq(i):
        pl.semaphore_signal(barrier, inc=1, device_id=(dp, (seq + i) % N_SEQ), device_id_type=MESH)

    def greet_dp(i):
        other_dp = (dp + i) % N_DP
        pl.semaphore_signal(barrier, inc=1, device_id=(other_dp, seq), device_id_type=MESH)
        pl.semaphore_signal(
            barrier, inc=1, device_id=(other_dp, z * 2 + 1 - yl), device_id_type=MESH
        )

    for i in range(1, N_SEQ):
        greet_seq(i)
    for i in range(1, N_DP):
        greet_dp(i)
    load_w(0).start()
    loads[1].start()
    for n in range(1, C_OUT // TILE):
        load_w(n).start()
    for load in loads[2:]:
        load.start()
    for load in small_loads:
        load.wait()
    own_row = jnp.concatenate([acceptor_v[...], jnp.full((1, 64), -1, I32)], axis=1)
    pos_own[...] = jnp.broadcast_to(own_row, (8, 128))
    loads[0].wait()
    pl.semaphore_wait(barrier, N_SEQ - 1 + 2 * (N_DP - 1))


    def halo_left():
        return pltpu.make_async_remote_copy(
            c_ext.at[pl.ds(0, 16)], halo_next, halo_ssem.at[0], halo_rsem.at[0],
            device_id=(dp, (seq + N_SEQ - 1) % N_SEQ), device_id_type=MESH)

    def halo_right():
        return pltpu.make_async_remote_copy(
            c_ext.at[pl.ds(COARSE - 16, 16)], halo_prev, halo_ssem.at[1], halo_rsem.at[1],
            device_id=(dp, (seq + 1) % N_SEQ), device_id_type=MESH)

    when(seq > 0, lambda: halo_left().start())
    when(seq < N_SEQ - 1, lambda: halo_right().start())
    drains.append(lambda: when(seq > 0, lambda: halo_left().wait_send()))
    drains.append(lambda: when(seq < N_SEQ - 1, lambda: halo_right().wait_send()))

    def pos_copy(i):
        return pltpu.make_async_remote_copy(
            pos_own, pos_all.at[seq], pos_ssem.at[i], pos_rsem.at[seq],
            device_id=(dp, (seq + i) % N_SEQ), device_id_type=MESH)

    def pos_start(i, carry):
        pos_copy(i).start()
        return carry

    lax.fori_loop(1, N_SEQ, pos_start, 0)
    drains.append(
        lambda: lax.fori_loop(1, N_SEQ, lambda i, carry: (pos_copy(i).wait_send(), carry)[1], 0)
    )
    pos_all[seq] = pos_own[...]

    loads[1].wait()
    at = iota((COARSE, FINE), 1)
    step2 = 2 * iota((COARSE, FINE), 0)
    even, odd = one_hot(at == step2), one_hot(at == step2 + 1)
    skip_f[pl.ds(0, COARSE)] = dot(even, skip_in[...]).astype(BF16)
    skip_f[pl.ds(COARSE, COARSE)] = dot(odd, skip_in[...]).astype(BF16)

    sub, lane = iota((128, 128), 0), iota((128, 128), 1)
    before = one_hot(sub < lane)
    place = sub % ACAP
    own = jnp.broadcast_to(own_row, (128, 128))
    own_hit = (own >> 9) == sub // ACAP
    own_rank = dot(one_hot(own_hit), before).astype(I32)
    to_served = jnp.where(own_hit & (own_rank == place), 1.0, 0.0)
    from_served = jnp.transpose(to_served)[:SLOTS].astype(BF16)
    to_served = to_served[:, :SLOTS].astype(BF16)
    pad = jnp.full((1, 64), -1, I32)
    donor_row = folded(jnp.concatenate([donor_v[...], pad], axis=1))
    donor_column = as_column(donor_row.astype(F32)).astype(I32)[:SLOTS]
    from_donor = one_hot(iota((SLOTS, FINE), 1) == donor_column)
    to_donor = one_hot(iota((FINE, 128), 0) == donor_row)
    fpad = jnp.zeros((1, 64), F32)
    mask_column = as_column(jnp.concatenate([mask_v[...].astype(F32), fpad], axis=1))[:SLOTS]
    score_column = as_column(jnp.concatenate([score_v[...], fpad], axis=1))[:SLOTS]
    weighted = score_column * mask_column

    when(seq < N_SEQ - 1, lambda: halo_left().wait_recv())
    when(seq > 0, lambda: halo_right().wait_recv())

    row16 = iota((16, C_IN), 0)
    c_ext[pl.ds(COARSE, 16)] = jnp.where(
        row16 == 0, halo_next[...].astype(F32),
        jnp.where(row16 == 15, halo_prev[...].astype(F32), 0.0),
    ).astype(BF16)

    def conv_tile(n, carry):
        load_w(n).wait()
        cols = pl.ds(pl.multiple_of(n * TILE, TILE), TILE)
        cells = c_ext[...]
        taps = [dot(cells, w[k, :, cols]) for k in range(TAPS)]
        even_sum = (
            pltpu.roll(taps[0] + taps[1], 1, 0) + taps[2] + taps[3] + pltpu.roll(taps[4], EXT - 1, 0)
        )
        odd_sum = (
            pltpu.roll(taps[0], 1, 0) + taps[1] + taps[2] + pltpu.roll(taps[3] + taps[4], EXT - 1, 0)
        )
        for part, total in ((0, even_sum), (1, odd_sum)):
            rows = pl.ds(part * COARSE, COARSE)
            v = total[:COARSE] + skip_f[rows, cols].astype(F32)
            square = v * v
            t = jnp.tanh(K0 * v * (1.0 + K1 * square))
            half = 0.5 * (1.0 + t)
            act[rows, cols] = (v * half).astype(BF16)
            slope[rows, cols] = half + 0.5 * v * (1.0 - t * t) * (K0 * (1.0 + 3.0 * K1 * square))
        return carry

    lax.fori_loop(0, C_OUT // TILE, conv_tile, 0)

    def pos_wait(i, carry):
        src = (seq + i) % N_SEQ
        pltpu.make_async_remote_copy(
            pos_own, pos_all.at[src], pos_ssem.at[i], pos_rsem.at[src],
            device_id=(dp, src), device_id_type=MESH).wait_recv()
        return carry

    lax.fori_loop(1, N_SEQ, pos_wait, 0)
    named = pos_all[...].reshape(CAP, 128)
    hit = (named >> 9) == seq
    rank = dot(one_hot(hit), before).astype(I32)
    chosen = jnp.where(hit & (rank == place), (named & (FINE - 1)) + 1, 0).astype(F32)
    served = jnp.sum(chosen, axis=1, keepdims=True).astype(I32) - 1
    served = folded(served)
    from_rows = one_hot(iota((CAP, FINE), 1) == served)
    served_row = as_row(served.astype(F32)).astype(I32)
    to_rows = one_hot(iota((FINE, CAP), 0) == served_row)
    a1_send[...] = pack(dot(from_rows, act[...]))

    def exchange(send, recv, ssem, rsem):
        def copy(i):
            peer = (seq + i) % N_SEQ
            return pltpu.make_async_remote_copy(
                send.at[peer], recv.at[seq], ssem.at[i], rsem.at[seq],
                device_id=(dp, peer), device_id_type=MESH)

        def start(i, carry):
            copy(i).start()
            return carry

        def wait(i, carry):
            src = (seq + i) % N_SEQ
            pltpu.make_async_remote_copy(
                send.at[src], recv.at[src], ssem.at[i], rsem.at[src],
                device_id=(dp, src), device_id_type=MESH).wait_recv()
            return carry

        def drain(i, carry):
            copy(i).wait_send()
            return carry

        return [lambda f=f: lax.fori_loop(1, N_SEQ, f, 0) for f in (start, wait, drain)]

    a1_start, a1_wait, a1_drain = exchange(a1_send, a1_recv, a1_ssem, a1_rsem)
    a2_start, a2_wait, a2_drain = exchange(a2_send, a2_recv, a2_ssem, a2_rsem)
    a1_start()
    drains.append(a1_drain)
    a1_recv[seq] = a1_send[seq]

    acts, grads = (dact, aact), (dgrad, agrad)
    ring_at = (x, y)
    first = jnp.where(core == 0, x, y)
    second = jnp.where(core == 0, y, x)
    active = first < 3

    def target(ring, p):
        if ring == 0:
            return (p * 4 + yh * 2, seq)
        return (x * 4 + (p // 2) * 2 + 1, z * 2 + p % 2)

    def act_copy(ring, p, source):
        kind = BLOCKS[ring][p][0]
        return pltpu.make_async_remote_copy(
            acts[kind], f_act.at[source], f_ssem.at[ring * 3 + p], f_rsem.at[source],
            device_id=target(ring, p), device_id_type=MESH)

    def grad_copy(ring, p, source):
        kind, block = BLOCKS[ring][p]
        return pltpu.make_async_remote_copy(
            grads[kind].at[:, pl.ds(block * BLOCK, BLOCK)], f_grad.at[source],
            g_ssem.at[ring * 3 + p], g_rsem.at[source],
            device_id=target(ring, p), device_id_type=MESH)

    def give_factor(kind, copy_of, keep):
        for ring in range(2):
            source = ring_at[ring] * 2 + core
            for p in range(3):
                if BLOCKS[ring][p][0] != kind:
                    continue
                mine = (core == ring) & (ring_at[ring] == p)
                when(jnp.logical_not(mine), lambda: copy_of(ring, p, source).start())
                when(mine, lambda: keep(source, BLOCKS[ring][p][1]))
                drains.append(
                    lambda ring=ring, p=p, mine=mine: when(
                        jnp.logical_not(mine), lambda: copy_of(ring, p, 0).wait_send()
                    )
                )

    def give_act(kind):
        def keep(source, block):
            f_act[source] = acts[kind][...]

        give_factor(kind, act_copy, keep)

    def give_grad(kind):
        def keep(source, block):
            f_grad[source] = grads[kind][:, block * BLOCK:(block + 1) * BLOCK]

        give_factor(kind, grad_copy, keep)

    loads[2].wait()
    loads[3].wait()
    donor_act = dot(from_donor, act[...]).astype(BF16)
    donor_emb = dot(donor_act, wd[...]).astype(BF16).astype(F32)
    acceptor_emb_grad = (weighted * donor_emb * INV_ROOT).astype(BF16)
    acceptor_rows = dot_nt(acceptor_emb_grad, wa[...]).astype(BF16)
    a2_send[...] = pack(dot(to_served, acceptor_rows))
    dact[...] = donor_act
    agrad[...] = acceptor_emb_grad
    give_act(0)
    give_grad(1)

    loads[4].wait()
    other_f[pl.ds(0, COARSE)] = dot(even, other_in[...]).astype(BF16)
    other_f[pl.ds(COARSE, COARSE)] = dot(odd, other_in[...]).astype(BF16)

    a1_wait()
    acceptor_act = dot(from_served, unpack(a1_recv[...])).astype(BF16)
    aact[...] = acceptor_act
    give_act(1)
    acceptor_emb = dot(acceptor_act, wa[...]).astype(BF16).astype(F32)
    score = mask_column * jnp.sum(donor_emb * acceptor_emb, axis=1, keepdims=True) * INV_ROOT
    score = jnp.concatenate([score, jnp.zeros((128 - SLOTS, 1), F32)], axis=0)
    scores_out[...] = as_row(score)[:, :SLOTS]
    donor_emb_grad = (weighted * acceptor_emb * INV_ROOT).astype(BF16)
    dgrad[...] = donor_emb_grad
    give_grad(0)
    a2_start()
    drains.append(a2_drain)
    a2_recv[seq] = a2_send[seq]

    sources = 8

    def second_device(r):
        if_donor = x * 4 + (r // 2) * 2
        if_acceptor = r * 4 + yh * 2 + 1
        return (
            jnp.where(core == 0, if_donor, if_acceptor),
            jnp.where(core == 0, z * 2 + r % 2, seq),
        )

    def chunk_copy(r, source):
        return pltpu.make_async_remote_copy(
            sum1.at[r // 2, :, r % 2], part2.at[source],
            s2_ssem.at[r], s2_rsem.at[source], device_id=second_device(r), device_id_type=MESH)

    def z_device(zt):
        return (dp, zt * 2 + yl)

    def z_copy(i):
        zt = (z + i) % N_Z
        return pltpu.make_async_remote_copy(
            sum2.at[zt], part3.at[z], s3_ssem.at[i], s3_rsem.at[z],
            device_id=z_device(zt), device_id_type=MESH)

    def of_block(i):
        value = 0
        for ring in range(2):
            for p in range(3):
                hit = (core == ring) & (first == p)
                value = jnp.where(hit, BLOCKS[ring][p][i], value)
        return value

    kind_at = of_block(0)
    tile_at = of_block(1) * 2 + second // 2
    seq_to = z * 2 + second % 2

    def gather_copy(d):
        return pltpu.make_async_remote_copy(
            piece, pieces.at[kind_at, tile_at], ag_ssem.at[d], ag_rsem.at[kind_at, tile_at],
            device_id=(d, seq_to), device_id_type=MESH)

    def block_sum():
        for s in range(sources):
            when(s != first * 2 + core, lambda: act_copy(0, 0, s).wait_recv())
        act_t[...] = jnp.transpose(f_act[...].reshape(sources * SLOTS, C_OUT))
        for s in range(sources):
            when(s != first * 2 + core, lambda: grad_copy(0, 0, s).wait_recv())
        for t in range(2):
            right = f_grad[:, :, t * 128:(t + 1) * 128].reshape(sources * SLOTS, 128)
            for m in range(2):
                block = dot(act_t[m * HALF:(m + 1) * HALF, :], right).astype(BF16)
                sum1[t, m * 4:(m + 1) * 4] = block.reshape(4, 2, ROWS_SEQ, 128)
            for r in (2 * t, 2 * t + 1):
                when(r != second, lambda: chunk_copy(r, second).start())

                @pl.when(r == second)
                def _(r=r):
                    part2[r] = sum1[r // 2, :, r % 2]

    def block_drain():
        for r in range(4):
            when(r != second, lambda: chunk_copy(r, second).wait_send())

    def ring_sum():
        for r in range(4):
            when(r != second, lambda: chunk_copy(r, r).wait_recv())
        sum2[...] = (
            part2[0].astype(F32) + part2[1].astype(F32) + part2[2].astype(F32) + part2[3].astype(F32)
        ).astype(BF16)
        for i in range(1, N_Z):
            z_copy(i).start()
        part3[z] = sum2[z]

    def ring_drain():
        for i in range(1, N_Z):
            z_copy(i).wait_send()

    def z_sum():
        for i in range(1, N_Z):
            src = (z + i) % N_Z
            pltpu.make_async_remote_copy(
                sum2.at[src], part3.at[src], s3_ssem.at[i], s3_rsem.at[src],
                device_id=z_device(src), device_id_type=MESH).wait_recv()
        total = part3[0].astype(F32)
        for i in range(1, N_Z):
            total = total + part3[i].astype(F32)
        piece[...] = (total * (1.0 / N_DP)).astype(BF16)
        for d in range(N_DP):
            mine = (d == dp) & (seq_to == seq)
            when(jnp.logical_not(mine), lambda: gather_copy(d).start())

            @pl.when(mine)
            def _(d=d):
                pieces[kind_at, tile_at] = piece[...]

    def z_drain():
        for d in range(N_DP):
            when(jnp.logical_not((d == dp) & (seq_to == seq)), lambda: gather_copy(d).wait_send())

    donor_rows = dot_nt(donor_emb_grad, wd[...]).astype(BF16)
    when(active, block_sum)
    drains.append(lambda: when(active, block_drain))

    a2_wait()
    served_rows = unpack(a2_recv[...])

    def grad_of(rows):
        total = (
            other_f[rows].astype(F32)
            + dot(to_rows[rows.start:rows.start + rows.size], served_rows)
            + dot(to_donor[rows.start:rows.start + rows.size, :SLOTS], donor_rows)
        )
        return total * slope[rows]

    g_even = grad_of(pl.ds(0, COARSE))
    g_odd = grad_of(pl.ds(COARSE, COARSE))
    pair = g_even + g_odd
    pe[pl.ds(0, COARSE)] = pair.astype(BF16)
    grad_left[pl.ds(0, 16)] = pair[:16].astype(BF16)
    grad_left[pl.ds(16, 16)] = g_even[:16].astype(BF16)
    grad_right[pl.ds(0, 16)] = pair[COARSE - 16:].astype(BF16)
    grad_right[pl.ds(16, 16)] = g_odd[COARSE - 16:].astype(BF16)

    def ghalo_left():
        return pltpu.make_async_remote_copy(
            grad_left, grad_next, ghalo_ssem.at[0], ghalo_rsem.at[0],
            device_id=(dp, (seq + N_SEQ - 1) % N_SEQ), device_id_type=MESH)

    def ghalo_right():
        return pltpu.make_async_remote_copy(
            grad_right, grad_prev, ghalo_ssem.at[1], ghalo_rsem.at[1],
            device_id=(dp, (seq + 1) % N_SEQ), device_id_type=MESH)

    when(seq > 0, lambda: ghalo_left().start())
    when(seq < N_SEQ - 1, lambda: ghalo_right().start())
    drains.append(lambda: when(seq > 0, lambda: ghalo_left().wait_send()))
    drains.append(lambda: when(seq < N_SEQ - 1, lambda: ghalo_right().wait_send()))

    shifted = pltpu.roll(g_odd, 1, 0)
    po[pl.ds(0, COARSE)] = (shifted + g_even).astype(BF16)

    when(seq < N_SEQ - 1, lambda: ghalo_left().wait_recv())
    when(seq > 0, lambda: ghalo_right().wait_recv())

    grow = iota((16, C_OUT), 0)
    after = grad_next[...].astype(F32)
    prior = grad_prev[...].astype(F32)
    pe[pl.ds(COARSE, 16)] = jnp.where(
        grow == 0, after[:16], jnp.where(grow == 15, prior[:16], 0.0)
    ).astype(BF16)
    prior_odd = pltpu.roll(prior[16:], 1, 0)
    po[pl.ds(0, 16)] = (
        jnp.where(grow == 0, prior_odd, shifted[:16]) + g_even[:16]
    ).astype(BF16)
    last_odd = pltpu.roll(g_odd[COARSE - 16:], 1, 0)
    po[pl.ds(COARSE, 16)] = jnp.where(grow == 0, last_odd + after[16:], 0.0).astype(BF16)

    when(active, ring_sum)
    drains.append(lambda: when(active, ring_drain))

    def back_tile(n, carry):
        cols = pl.ds(pl.multiple_of(n * TILE, TILE), TILE)
        pairs, cross = pe[...], po[...]
        ahead = dot_nt(pairs, w[0, cols, :]) + dot_nt(cross, w[1, cols, :])
        here = dot_nt(pairs[:COARSE], w[2, cols, :]) + dot_nt(cross[:COARSE], w[3, cols, :])
        behind = dot_nt(pairs, w[4, cols, :])
        total = here + pltpu.roll(ahead, EXT - 1, 0)[:COARSE] + pltpu.roll(behind, 1, 0)[:COARSE]
        coarse_out[0, :, cols] = total.astype(BF16)
        return carry

    lax.fori_loop(0, C_IN // TILE, back_tile, 0)
    when(active, z_sum)
    drains.append(lambda: when(active, z_drain))

    for kind, out in ((0, donor_out), (1, acceptor_out)):
        for t in range(6):
            ring = 0 if (kind, t // 2) in BLOCKS[0] else 1
            p = BLOCKS[ring].index((kind, t // 2))
            if ring == 0:
                source = (p * 4 + (t % 2) * 2, seq)
            else:
                source = (((t % 2) * 2 + yl) * 4 + (p // 2) * 2 + 1, z * 2 + p % 2)
            mine = (source[0] == dp) & (source[1] == seq)

            @pl.when(jnp.logical_not(mine))
            def _(kind=kind, t=t, source=source):
                pltpu.make_async_remote_copy(
                    piece, pieces.at[kind, t], ag_ssem.at[0], ag_rsem.at[kind, t],
                    device_id=source, device_id_type=MESH).wait_recv()

            out[:, t * 128:(t + 1) * 128] = pieces[kind, t].astype(F32)

    finish()


def write_out(*refs):
    sem = refs[8]
    copies = [pltpu.make_async_copy(refs[i], refs[4 + i], sem.at[i]) for i in range(4)]
    for copy in copies:
        copy.start()
    for copy in copies:
        copy.wait()


def on_device(*args):
    vmem = pl.BlockSpec(memory_space=pltpu.VMEM)
    hbm = pl.BlockSpec(memory_space=pltpu.HBM)
    dma = pltpu.SemaphoreType.DMA

    def v(*shape, dtype=BF16):
        return pltpu.VMEM(shape, dtype)

    scratch = [
        v(1, SLOTS, dtype=F32), v(1, SLOTS, dtype=I32), v(1, SLOTS, dtype=I32), v(1, SLOTS, dtype=I32),
        v(TAPS, C_IN, C_OUT), v(C_OUT, EMB), v(C_OUT, EMB), v(EXT, C_IN),
        v(FINE, C_OUT), v(FINE, C_OUT), v(FINE, C_OUT), v(FINE, C_OUT),
        v(FINE, C_OUT), v(FINE, C_OUT, dtype=F32),
        v(16, C_IN), v(16, C_IN), v(32, C_OUT), v(32, C_OUT), v(32, C_OUT), v(32, C_OUT),
        v(8, 128, dtype=I32), v(N_SEQ, 8, 128, dtype=I32),
        v(N_SEQ, 16, HALF), v(N_SEQ, 16, HALF), v(N_SEQ, 16, HALF), v(N_SEQ, 16, HALF),
        v(EXT, C_OUT), v(EXT, C_OUT),
        v(SLOTS, C_OUT), v(SLOTS, EMB), v(SLOTS, C_OUT), v(SLOTS, EMB),
        v(8, SLOTS, C_OUT), v(8, SLOTS, BLOCK), v(2, N_Z, 2, ROWS_SEQ, 128), v(C_OUT, 8 * SLOTS),
        v(4, N_Z, ROWS_SEQ, 128), v(N_Z, ROWS_SEQ, 128), v(N_Z, ROWS_SEQ, 128),
        v(ROWS_SEQ, 128), v(2, 6, ROWS_SEQ, 128),
        dma((9,)), dma((3,)), dma((2,)), dma((2,)), dma((2,)), dma((2,)),
        dma((N_SEQ,)), dma((N_SEQ,)), dma((N_SEQ,)), dma((N_SEQ,)), dma((N_SEQ,)), dma((N_SEQ,)),
        dma((6,)), dma((8,)), dma((6,)), dma((8,)),
        dma((4,)), dma((4,)), dma((N_Z,)), dma((N_Z,)), dma((N_DP,)), dma((2, 6)),
    ]
    shapes = (
        jax.ShapeDtypeStruct((1, SLOTS), F32),
        jax.ShapeDtypeStruct((1, COARSE, C_IN), BF16),
        jax.ShapeDtypeStruct((ROWS_SEQ, EMB), F32),
        jax.ShapeDtypeStruct((ROWS_SEQ, EMB), F32),
    )
    args = [pltpu.with_memory_space_constraint(a, pltpu.HBM) for a in args]
    results = pl.pallas_call(
        kernel,
        out_shape=shapes,
        in_specs=[hbm] * 10,
        out_specs=(vmem,) * 4,
        scratch_shapes=scratch,
        compiler_params=pltpu.CompilerParams(
            collective_id=0, has_side_effects=True, vmem_limit_bytes=48*1024*1024
        ),
    )(*args)
    return pl.pallas_call(
        write_out,
        out_shape=shapes,
        in_specs=[vmem] * 4,
        out_specs=(pl.BlockSpec(memory_space=pl.ANY),) * 4,
        scratch_shapes=[dma((4,))],
        compiler_params=pltpu.CompilerParams(vmem_limit_bytes=1024 * 1024),
    )(*results)


def solution(mesh):
    rows, slots = P("dp", "seq", None), P("dp", "seq")
    return jax.shard_map(
        on_device,
        mesh=mesh,
        in_specs=(rows, rows, P(), P(), P(), rows, slots, slots, slots, slots),
        out_specs=(slots, rows, P("seq", None), P("seq", None)),
        check_vma=False,
    )
```

```python
import math

import jax
import jax.numpy as jnp
from jax import lax
from jax.experimental import pallas as pl
from jax.experimental.pallas import tpu as pltpu
from jax.sharding import PartitionSpec as P

MESH = pl.DeviceIdType.MESH
F32, BF16, I32 = jnp.float32, jnp.bfloat16, jnp.int32
N_X, N_Y, N_Z = 4, 4, 8
N_DP, N_SEQ = 16, 16
COARSE, FINE, C_IN, C_OUT, EMB = 256, 512, 1024, 768, 768
EXT = COARSE + 16
TAPS, ACAP, SLOTS = 5, 8, 64
CAP = N_SEQ * ACAP
TILE = 256
HALF = 384
BLOCKS = (((1, 2), (0, 0), (0, 1)), ((1, 0), (0, 2), (1, 1)))
FAR_SEQ = (8, 7, 9, 6, 10, 5, 11, 4, 12, 3, 13, 2, 14, 1, 15)
FAR_Z = (4, 3, 5, 2, 6, 1, 7)
FAR_DP = tuple(
    (dx, dy, dc) for dx, dy in ((2, 1), (2, 0), (1, 1), (3, 1), (0, 1), (1, 0), (3, 0)) for dc in (0, 1)
) + ((0, 0, 1),)
BLOCK = 256
ROWS_SEQ = C_OUT // N_SEQ
INV_ROOT = 1.0 / math.sqrt(EMB)
K0 = math.sqrt(2.0 / math.pi)
K1 = 0.044715


def dot(a, b):
    return jnp.dot(a, b, preferred_element_type=F32)


def dot_nt(a, b):
    return lax.dot_general(a, b, (((1,), (1,)), ((), ())), preferred_element_type=F32)


def dot_tn(a, b):
    return lax.dot_general(a, b, (((0,), (0,)), ((), ())), preferred_element_type=F32)


def one_hot(condition):
    return jnp.where(condition, 1.0, 0.0).astype(BF16)


def iota(shape, axis):
    return lax.broadcasted_iota(I32, shape, axis)


def as_column(row):
    return jnp.transpose(jnp.broadcast_to(row, (128, 128)))[:, 0:1]


def as_row(column):
    return jnp.transpose(jnp.broadcast_to(column, (128, 128)))[0:1, :]


def folded(row):
    return jnp.where(row < 0, -1, (row & 1) * COARSE + (row >> 1))


def pack(rows):
    cells = rows.reshape(N_SEQ, ACAP, EMB)
    return jnp.concatenate([cells[:, :, :HALF], cells[:, :, HALF:]], axis=1).astype(BF16)


def unpack(cells):
    wide = cells.astype(F32)
    both = jnp.concatenate([wide[:, :ACAP], wide[:, ACAP:]], axis=2)
    return both.reshape(CAP, EMB).astype(BF16)


def kernel(
    coarse, skip, conv_w, donor_w, acceptor_w, other, score_grad, donor_pos, acceptor_pos, mask,
    scores_out, coarse_out, donor_out, acceptor_out,
    score_v, donor_v, acceptor_v, mask_v, w, wd, wa, c_ext, skip_in, other_in, skip_f, other_f, act, slope,
    halo_next, halo_prev, grad_next, grad_prev, grad_left, grad_right,
    pos_own, pos_all, a1_send, a1_recv, a2_send, a2_recv,
    pe, po, dact, dgrad, aact, agrad,
    f_act, f_grad, sum1, act_t, part2, sum2, part3, piece, pieces,
    load_sem, w_sem, halo_ssem, halo_rsem, ghalo_ssem, ghalo_rsem,
    pos_ssem, pos_rsem, a1_ssem, a1_rsem, a2_ssem, a2_rsem,
    f_ssem, f_rsem, g_ssem, g_rsem,
    s2_ssem, s2_rsem, s3_ssem, s3_rsem, ag_ssem, ag_rsem,
):
    dp, seq = lax.axis_index("dp"), lax.axis_index("seq")
    x, yh, core = dp // 4, (dp // 2) % 2, dp % 2
    z, yl = seq // 2, seq % 2
    y = yh * 2 + yl

    drains = []

    def finish():
        for drain in drains:
            drain()

    def when(condition, action):
        pl.when(condition)(action)

    smalls = (score_grad, donor_pos, acceptor_pos, mask)
    held = (score_v, donor_v, acceptor_v, mask_v)
    small_loads = [
        pltpu.make_async_copy(a, b, load_sem.at[5 + i]) for i, (a, b) in enumerate(zip(smalls, held))
    ]
    loads = [
        pltpu.make_async_copy(coarse.at[0], c_ext.at[pl.ds(0, COARSE)], load_sem.at[0]),
        pltpu.make_async_copy(skip.at[0], skip_in, load_sem.at[1]),
        pltpu.make_async_copy(donor_w, wd, load_sem.at[2]),
        pltpu.make_async_copy(acceptor_w, wa, load_sem.at[3]),
        pltpu.make_async_copy(other.at[0], other_in, load_sem.at[4]),
    ]

    def load_w(n):
        cols = pl.ds(pl.multiple_of(n * TILE, TILE), TILE)
        return pltpu.make_async_copy(conv_w.at[:, :, cols], w.at[:, :, cols], w_sem.at[n])

    for load in small_loads:
        load.start()
    loads[0].start()

    halo_next[...] = jnp.zeros_like(halo_next)
    halo_prev[...] = jnp.zeros_like(halo_prev)
    grad_next[...] = jnp.zeros_like(grad_next)
    grad_prev[...] = jnp.zeros_like(grad_prev)
    barrier = pltpu.get_barrier_semaphore()

    def greet_seq(i):
        pl.semaphore_signal(barrier, inc=1, device_id=(dp, (seq + i) % N_SEQ), device_id_type=MESH)

    def greet_dp(i):
        other_dp = (dp + i) % N_DP
        pl.semaphore_signal(barrier, inc=1, device_id=(other_dp, seq), device_id_type=MESH)
        pl.semaphore_signal(
            barrier, inc=1, device_id=(other_dp, z * 2 + 1 - yl), device_id_type=MESH
        )

    for i in range(1, N_SEQ):
        greet_seq(i)
    for i in range(1, N_DP):
        greet_dp(i)
    load_w(0).start()
    loads[1].start()
    for n in range(1, C_OUT // TILE):
        load_w(n).start()
    for load in loads[2:]:
        load.start()
    for load in small_loads:
        load.wait()
    own_row = jnp.concatenate([acceptor_v[...], jnp.full((1, 64), -1, I32)], axis=1)
    pos_own[...] = jnp.broadcast_to(own_row, (8, 128))
    loads[0].wait()
    pl.semaphore_wait(barrier, N_SEQ - 1 + 2 * (N_DP - 1))


    def halo_left():
        return pltpu.make_async_remote_copy(
            c_ext.at[pl.ds(0, 16)], halo_next, halo_ssem.at[0], halo_rsem.at[0],
            device_id=(dp, (seq + N_SEQ - 1) % N_SEQ), device_id_type=MESH)

    def halo_right():
        return pltpu.make_async_remote_copy(
            c_ext.at[pl.ds(COARSE - 16, 16)], halo_prev, halo_ssem.at[1], halo_rsem.at[1],
            device_id=(dp, (seq + 1) % N_SEQ), device_id_type=MESH)

    when(seq > 0, lambda: halo_left().start())
    when(seq < N_SEQ - 1, lambda: halo_right().start())
    drains.append(lambda: when(seq > 0, lambda: halo_left().wait_send()))
    drains.append(lambda: when(seq < N_SEQ - 1, lambda: halo_right().wait_send()))

    def pos_copy(i):
        return pltpu.make_async_remote_copy(
            pos_own, pos_all.at[seq], pos_ssem.at[i], pos_rsem.at[seq],
            device_id=(dp, (seq + i) % N_SEQ), device_id_type=MESH)

    for i in FAR_SEQ:
        pos_copy(i).start()
    drains.append(
        lambda: lax.fori_loop(1, N_SEQ, lambda i, carry: (pos_copy(i).wait_send(), carry)[1], 0)
    )
    pos_all[seq] = pos_own[...]

    loads[1].wait()
    at = iota((COARSE, FINE), 1)
    step2 = 2 * iota((COARSE, FINE), 0)
    even, odd = one_hot(at == step2), one_hot(at == step2 + 1)
    skip_f[pl.ds(0, COARSE)] = dot(even, skip_in[...]).astype(BF16)
    skip_f[pl.ds(COARSE, COARSE)] = dot(odd, skip_in[...]).astype(BF16)

    sub, lane = iota((128, 128), 0), iota((128, 128), 1)
    before = one_hot(sub < lane)
    place = sub % ACAP
    own = jnp.broadcast_to(own_row, (128, 128))
    own_hit = (own >> 9) == sub // ACAP
    own_rank = dot(one_hot(own_hit), before).astype(I32)
    to_served = jnp.where(own_hit & (own_rank == place), 1.0, 0.0)
    from_served = jnp.transpose(to_served)[:SLOTS].astype(BF16)
    to_served = to_served[:, :SLOTS].astype(BF16)
    pad = jnp.full((1, 64), -1, I32)
    donor_row = folded(jnp.concatenate([donor_v[...], pad], axis=1))
    donor_column = as_column(donor_row.astype(F32)).astype(I32)[:SLOTS]
    from_donor = one_hot(iota((SLOTS, FINE), 1) == donor_column)
    to_donor = one_hot(iota((FINE, 128), 0) == donor_row)
    fpad = jnp.zeros((1, 64), F32)
    mask_column = as_column(jnp.concatenate([mask_v[...].astype(F32), fpad], axis=1))[:SLOTS]
    score_column = as_column(jnp.concatenate([score_v[...], fpad], axis=1))[:SLOTS]
    weighted = score_column * mask_column

    when(seq < N_SEQ - 1, lambda: halo_left().wait_recv())
    when(seq > 0, lambda: halo_right().wait_recv())

    row16 = iota((16, C_IN), 0)
    c_ext[pl.ds(COARSE, 16)] = jnp.where(
        row16 == 0, halo_next[...].astype(F32),
        jnp.where(row16 == 15, halo_prev[...].astype(F32), 0.0),
    ).astype(BF16)

    def conv_tile(n, carry):
        load_w(n).wait()
        cols = pl.ds(pl.multiple_of(n * TILE, TILE), TILE)
        cells = c_ext[...]
        taps = [dot(cells, w[k, :, cols]) for k in range(TAPS)]
        even_sum = (
            pltpu.roll(taps[0] + taps[1], 1, 0) + taps[2] + taps[3] + pltpu.roll(taps[4], EXT - 1, 0)
        )
        odd_sum = (
            pltpu.roll(taps[0], 1, 0) + taps[1] + taps[2] + pltpu.roll(taps[3] + taps[4], EXT - 1, 0)
        )
        for part, total in ((0, even_sum), (1, odd_sum)):
            rows = pl.ds(part * COARSE, COARSE)
            v = total[:COARSE] + skip_f[rows, cols].astype(F32)
            square = v * v
            t = jnp.tanh(K0 * v * (1.0 + K1 * square))
            half = 0.5 * (1.0 + t)
            act[rows, cols] = (v * half).astype(BF16)
            slope[rows, cols] = half + 0.5 * v * (1.0 - t * t) * (K0 * (1.0 + 3.0 * K1 * square))
        return carry

    lax.fori_loop(0, C_OUT // TILE, conv_tile, 0)

    def pos_wait(i, carry):
        src = (seq + i) % N_SEQ
        pltpu.make_async_remote_copy(
            pos_own, pos_all.at[src], pos_ssem.at[i], pos_rsem.at[src],
            device_id=(dp, src), device_id_type=MESH).wait_recv()
        return carry

    lax.fori_loop(1, N_SEQ, pos_wait, 0)
    named = pos_all[...].reshape(CAP, 128)
    hit = (named >> 9) == seq
    rank = dot(one_hot(hit), before).astype(I32)
    chosen = jnp.where(hit & (rank == place), (named & (FINE - 1)) + 1, 0).astype(F32)
    served = jnp.sum(chosen, axis=1, keepdims=True).astype(I32) - 1
    served = folded(served)
    from_rows = one_hot(iota((CAP, FINE), 1) == served)
    served_row = as_row(served.astype(F32)).astype(I32)
    to_rows = one_hot(iota((FINE, CAP), 0) == served_row)
    a1_send[...] = pack(dot(from_rows, act[...]))

    def exchange(send, recv, ssem, rsem):
        def copy(i):
            peer = (seq + i) % N_SEQ
            return pltpu.make_async_remote_copy(
                send.at[peer], recv.at[seq], ssem.at[i], rsem.at[seq],
                device_id=(dp, peer), device_id_type=MESH)

        def start():
            for i in FAR_SEQ:
                copy(i).start()

        def wait(i, carry):
            src = (seq + i) % N_SEQ
            pltpu.make_async_remote_copy(
                send.at[src], recv.at[src], ssem.at[i], rsem.at[src],
                device_id=(dp, src), device_id_type=MESH).wait_recv()
            return carry

        def drain(i, carry):
            copy(i).wait_send()
            return carry

        return [start] + [lambda f=f: lax.fori_loop(1, N_SEQ, f, 0) for f in (wait, drain)]

    a1_start, a1_wait, a1_drain = exchange(a1_send, a1_recv, a1_ssem, a1_rsem)
    a2_start, a2_wait, a2_drain = exchange(a2_send, a2_recv, a2_ssem, a2_rsem)
    a1_start()
    drains.append(a1_drain)
    a1_recv[seq] = a1_send[seq]

    acts, grads = (dact, aact), (dgrad, agrad)
    ring_at = (x, y)
    first = jnp.where(core == 0, x, y)
    second = jnp.where(core == 0, y, x)
    active = first < 3

    def target(ring, p):
        if ring == 0:
            return (p * 4 + yh * 2, seq)
        return (x * 4 + (p // 2) * 2 + 1, z * 2 + p % 2)

    def act_copy(ring, p, source):
        kind = BLOCKS[ring][p][0]
        return pltpu.make_async_remote_copy(
            acts[kind], f_act.at[source], f_ssem.at[ring * 3 + p], f_rsem.at[source],
            device_id=target(ring, p), device_id_type=MESH)

    def grad_copy(ring, p, source):
        kind, block = BLOCKS[ring][p]
        return pltpu.make_async_remote_copy(
            grads[kind].at[:, pl.ds(block * BLOCK, BLOCK)], f_grad.at[source],
            g_ssem.at[ring * 3 + p], g_rsem.at[source],
            device_id=target(ring, p), device_id_type=MESH)

    def give_factor(kind, copy_of, keep):
        for ring in range(2):
            source = ring_at[ring] * 2 + core
            for p in range(3):
                if BLOCKS[ring][p][0] != kind:
                    continue
                mine = (core == ring) & (ring_at[ring] == p)
                when(jnp.logical_not(mine), lambda: copy_of(ring, p, source).start())
                when(mine, lambda: keep(source, BLOCKS[ring][p][1]))
                drains.append(
                    lambda ring=ring, p=p, mine=mine: when(
                        jnp.logical_not(mine), lambda: copy_of(ring, p, 0).wait_send()
                    )
                )

    def give_act(kind):
        def keep(source, block):
            f_act[source] = acts[kind][...]

        give_factor(kind, act_copy, keep)

    def give_grad(kind):
        def keep(source, block):
            f_grad[source] = grads[kind][:, block * BLOCK:(block + 1) * BLOCK]

        give_factor(kind, grad_copy, keep)

    loads[2].wait()
    loads[3].wait()
    donor_act = dot(from_donor, act[...]).astype(BF16)
    donor_emb = dot(donor_act, wd[...]).astype(BF16).astype(F32)
    acceptor_emb_grad = (weighted * donor_emb * INV_ROOT).astype(BF16)
    acceptor_rows = dot_nt(acceptor_emb_grad, wa[...]).astype(BF16)
    a2_send[...] = pack(dot(to_served, acceptor_rows))
    dact[...] = donor_act
    agrad[...] = acceptor_emb_grad
    give_act(0)
    give_grad(1)

    loads[4].wait()
    other_f[pl.ds(0, COARSE)] = dot(even, other_in[...]).astype(BF16)
    other_f[pl.ds(COARSE, COARSE)] = dot(odd, other_in[...]).astype(BF16)

    a1_wait()
    acceptor_act = dot(from_served, unpack(a1_recv[...])).astype(BF16)
    aact[...] = acceptor_act
    give_act(1)
    acceptor_emb = dot(acceptor_act, wa[...]).astype(BF16).astype(F32)
    score = mask_column * jnp.sum(donor_emb * acceptor_emb, axis=1, keepdims=True) * INV_ROOT
    score = jnp.concatenate([score, jnp.zeros((128 - SLOTS, 1), F32)], axis=0)
    scores_out[...] = as_row(score)[:, :SLOTS]
    donor_emb_grad = (weighted * acceptor_emb * INV_ROOT).astype(BF16)
    dgrad[...] = donor_emb_grad
    give_grad(0)
    a2_start()
    drains.append(a2_drain)
    a2_recv[seq] = a2_send[seq]

    sources = 8

    def second_device(r):
        if_donor = x * 4 + (r // 2) * 2
        if_acceptor = r * 4 + yh * 2 + 1
        return (
            jnp.where(core == 0, if_donor, if_acceptor),
            jnp.where(core == 0, z * 2 + r % 2, seq),
        )

    def chunk_copy(r, source):
        return pltpu.make_async_remote_copy(
            sum1.at[r // 2, :, r % 2], part2.at[source],
            s2_ssem.at[r], s2_rsem.at[source], device_id=second_device(r), device_id_type=MESH)

    def z_device(zt):
        return (dp, zt * 2 + yl)

    def z_copy(i):
        zt = (z + i) % N_Z
        return pltpu.make_async_remote_copy(
            sum2.at[zt], part3.at[z], s3_ssem.at[i], s3_rsem.at[z],
            device_id=z_device(zt), device_id_type=MESH)

    def of_block(i):
        value = 0
        for ring in range(2):
            for p in range(3):
                hit = (core == ring) & (first == p)
                value = jnp.where(hit, BLOCKS[ring][p][i], value)
        return value

    kind_at = of_block(0)
    tile_at = of_block(1) * 2 + second // 2
    seq_to = z * 2 + second % 2

    def dp_at(dx, dy, dc):
        return ((x + dx) % N_X) * 4 + ((yh + dy) % 2) * 2 + (core + dc) % 2

    def gather_copy(d):
        return pltpu.make_async_remote_copy(
            piece, pieces.at[kind_at, tile_at], ag_ssem.at[d], ag_rsem.at[kind_at, tile_at],
            device_id=(d, seq_to), device_id_type=MESH)

    def block_sum():
        for s in range(sources):
            when(s != first * 2 + core, lambda: act_copy(0, 0, s).wait_recv())
        act_t[...] = jnp.transpose(f_act[...].reshape(sources * SLOTS, C_OUT))
        for s in range(sources):
            when(s != first * 2 + core, lambda: grad_copy(0, 0, s).wait_recv())
        for t in range(2):
            right = f_grad[:, :, t * 128:(t + 1) * 128].reshape(sources * SLOTS, 128)
            for m in range(2):
                block = dot(act_t[m * HALF:(m + 1) * HALF, :], right).astype(BF16)
                sum1[t, m * 4:(m + 1) * 4] = block.reshape(4, 2, ROWS_SEQ, 128)
            for r in (2 * t, 2 * t + 1):
                when(r != second, lambda: chunk_copy(r, second).start())

                @pl.when(r == second)
                def _(r=r):
                    part2[r] = sum1[r // 2, :, r % 2]

    def block_drain():
        for r in range(4):
            when(r != second, lambda: chunk_copy(r, second).wait_send())

    def ring_sum():
        for r in range(4):
            when(r != second, lambda: chunk_copy(r, r).wait_recv())
        sum2[...] = (
            part2[0].astype(F32) + part2[1].astype(F32) + part2[2].astype(F32) + part2[3].astype(F32)
        ).astype(BF16)
        for i in FAR_Z:
            z_copy(i).start()
        part3[z] = sum2[z]

    def ring_drain():
        for i in range(1, N_Z):
            z_copy(i).wait_send()

    def z_sum():
        for i in range(1, N_Z):
            src = (z + i) % N_Z
            pltpu.make_async_remote_copy(
                sum2.at[src], part3.at[src], s3_ssem.at[i], s3_rsem.at[src],
                device_id=z_device(src), device_id_type=MESH).wait_recv()
        total = part3[0].astype(F32)
        for i in range(1, N_Z):
            total = total + part3[i].astype(F32)
        piece[...] = (total * (1.0 / N_DP)).astype(BF16)
        for offset in FAR_DP:
            gather_copy(dp_at(*offset)).start()
        when(seq_to != seq, lambda: gather_copy(dp).start())

        @pl.when(seq_to == seq)
        def _():
            pieces[kind_at, tile_at] = piece[...]

    def z_drain():
        for offset in FAR_DP:
            gather_copy(dp_at(*offset)).wait_send()
        when(seq_to != seq, lambda: gather_copy(dp).wait_send())

    donor_rows = dot_nt(donor_emb_grad, wd[...]).astype(BF16)
    when(active, block_sum)
    drains.append(lambda: when(active, block_drain))

    a2_wait()
    served_rows = unpack(a2_recv[...])

    def grad_of(rows):
        total = (
            other_f[rows].astype(F32)
            + dot(to_rows[rows.start:rows.start + rows.size], served_rows)
            + dot(to_donor[rows.start:rows.start + rows.size, :SLOTS], donor_rows)
        )
        return total * slope[rows]

    g_even = grad_of(pl.ds(0, COARSE))
    g_odd = grad_of(pl.ds(COARSE, COARSE))
    pair = g_even + g_odd
    pe[pl.ds(0, COARSE)] = pair.astype(BF16)
    grad_left[pl.ds(0, 16)] = pair[:16].astype(BF16)
    grad_left[pl.ds(16, 16)] = g_even[:16].astype(BF16)
    grad_right[pl.ds(0, 16)] = pair[COARSE - 16:].astype(BF16)
    grad_right[pl.ds(16, 16)] = g_odd[COARSE - 16:].astype(BF16)

    def ghalo_left():
        return pltpu.make_async_remote_copy(
            grad_left, grad_next, ghalo_ssem.at[0], ghalo_rsem.at[0],
            device_id=(dp, (seq + N_SEQ - 1) % N_SEQ), device_id_type=MESH)

    def ghalo_right():
        return pltpu.make_async_remote_copy(
            grad_right, grad_prev, ghalo_ssem.at[1], ghalo_rsem.at[1],
            device_id=(dp, (seq + 1) % N_SEQ), device_id_type=MESH)

    when(seq > 0, lambda: ghalo_left().start())
    when(seq < N_SEQ - 1, lambda: ghalo_right().start())
    drains.append(lambda: when(seq > 0, lambda: ghalo_left().wait_send()))
    drains.append(lambda: when(seq < N_SEQ - 1, lambda: ghalo_right().wait_send()))

    shifted = pltpu.roll(g_odd, 1, 0)
    po[pl.ds(0, COARSE)] = (shifted + g_even).astype(BF16)

    when(seq < N_SEQ - 1, lambda: ghalo_left().wait_recv())
    when(seq > 0, lambda: ghalo_right().wait_recv())

    grow = iota((16, C_OUT), 0)
    after = grad_next[...].astype(F32)
    prior = grad_prev[...].astype(F32)
    pe[pl.ds(COARSE, 16)] = jnp.where(
        grow == 0, after[:16], jnp.where(grow == 15, prior[:16], 0.0)
    ).astype(BF16)
    prior_odd = pltpu.roll(prior[16:], 1, 0)
    po[pl.ds(0, 16)] = (
        jnp.where(grow == 0, prior_odd, shifted[:16]) + g_even[:16]
    ).astype(BF16)
    last_odd = pltpu.roll(g_odd[COARSE - 16:], 1, 0)
    po[pl.ds(COARSE, 16)] = jnp.where(grow == 0, last_odd + after[16:], 0.0).astype(BF16)

    when(active, ring_sum)
    drains.append(lambda: when(active, ring_drain))

    def back_tile(n, carry):
        cols = pl.ds(pl.multiple_of(n * TILE, TILE), TILE)
        pairs, cross = pe[...], po[...]
        ahead = dot_nt(pairs, w[0, cols, :]) + dot_nt(cross, w[1, cols, :])
        here = dot_nt(pairs[:COARSE], w[2, cols, :]) + dot_nt(cross[:COARSE], w[3, cols, :])
        behind = dot_nt(pairs, w[4, cols, :])
        total = here + pltpu.roll(ahead, EXT - 1, 0)[:COARSE] + pltpu.roll(behind, 1, 0)[:COARSE]
        coarse_out[0, :, cols] = total.astype(BF16)
        return carry

    lax.fori_loop(0, C_IN // TILE, back_tile, 0)
    when(active, z_sum)
    finish()

    for kind, out in ((0, donor_out), (1, acceptor_out)):
        for t in range(6):
            ring = 0 if (kind, t // 2) in BLOCKS[0] else 1
            p = BLOCKS[ring].index((kind, t // 2))
            if ring == 0:
                source = (p * 4 + (t % 2) * 2, seq)
            else:
                source = (((t % 2) * 2 + yl) * 4 + (p // 2) * 2 + 1, z * 2 + p % 2)
            mine = (source[0] == dp) & (source[1] == seq)

            @pl.when(jnp.logical_not(mine))
            def _(kind=kind, t=t, source=source):
                pltpu.make_async_remote_copy(
                    piece, pieces.at[kind, t], ag_ssem.at[0], ag_rsem.at[kind, t],
                    device_id=source, device_id_type=MESH).wait_recv()

            out[:, t * 128:(t + 1) * 128] = pieces[kind, t].astype(F32)

    when(active, z_drain)


def write_out(*refs):
    sem = refs[8]
    copies = [pltpu.make_async_copy(refs[i], refs[4 + i], sem.at[i]) for i in range(4)]
    for copy in copies:
        copy.start()
    for copy in copies:
        copy.wait()


def on_device(*args):
    vmem = pl.BlockSpec(memory_space=pltpu.VMEM)
    hbm = pl.BlockSpec(memory_space=pltpu.HBM)
    dma = pltpu.SemaphoreType.DMA

    def v(*shape, dtype=BF16):
        return pltpu.VMEM(shape, dtype)

    scratch = [
        v(1, SLOTS, dtype=F32), v(1, SLOTS, dtype=I32), v(1, SLOTS, dtype=I32), v(1, SLOTS, dtype=I32),
        v(TAPS, C_IN, C_OUT), v(C_OUT, EMB), v(C_OUT, EMB), v(EXT, C_IN),
        v(FINE, C_OUT), v(FINE, C_OUT), v(FINE, C_OUT), v(FINE, C_OUT),
        v(FINE, C_OUT), v(FINE, C_OUT, dtype=F32),
        v(16, C_IN), v(16, C_IN), v(32, C_OUT), v(32, C_OUT), v(32, C_OUT), v(32, C_OUT),
        v(8, 128, dtype=I32), v(N_SEQ, 8, 128, dtype=I32),
        v(N_SEQ, 16, HALF), v(N_SEQ, 16, HALF), v(N_SEQ, 16, HALF), v(N_SEQ, 16, HALF),
        v(EXT, C_OUT), v(EXT, C_OUT),
        v(SLOTS, C_OUT), v(SLOTS, EMB), v(SLOTS, C_OUT), v(SLOTS, EMB),
        v(8, SLOTS, C_OUT), v(8, SLOTS, BLOCK), v(2, N_Z, 2, ROWS_SEQ, 128), v(C_OUT, 8 * SLOTS),
        v(4, N_Z, ROWS_SEQ, 128), v(N_Z, ROWS_SEQ, 128), v(N_Z, ROWS_SEQ, 128),
        v(ROWS_SEQ, 128), v(2, 6, ROWS_SEQ, 128),
        dma((9,)), dma((3,)), dma((2,)), dma((2,)), dma((2,)), dma((2,)),
        dma((N_SEQ,)), dma((N_SEQ,)), dma((N_SEQ,)), dma((N_SEQ,)), dma((N_SEQ,)), dma((N_SEQ,)),
        dma((6,)), dma((8,)), dma((6,)), dma((8,)),
        dma((4,)), dma((4,)), dma((N_Z,)), dma((N_Z,)), dma((N_DP,)), dma((2, 6)),
    ]
    shapes = (
        jax.ShapeDtypeStruct((1, SLOTS), F32),
        jax.ShapeDtypeStruct((1, COARSE, C_IN), BF16),
        jax.ShapeDtypeStruct((ROWS_SEQ, EMB), F32),
        jax.ShapeDtypeStruct((ROWS_SEQ, EMB), F32),
    )
    args = [pltpu.with_memory_space_constraint(a, pltpu.HBM) for a in args]
    results = pl.pallas_call(
        kernel,
        out_shape=shapes,
        in_specs=[hbm] * 10,
        out_specs=(vmem,) * 4,
        scratch_shapes=scratch,
        compiler_params=pltpu.CompilerParams(
            collective_id=0, has_side_effects=True, vmem_limit_bytes=48*1024*1024
        ),
    )(*args)
    return pl.pallas_call(
        write_out,
        out_shape=shapes,
        in_specs=[vmem] * 4,
        out_specs=(pl.BlockSpec(memory_space=pl.ANY),) * 4,
        scratch_shapes=[dma((4,))],
        compiler_params=pltpu.CompilerParams(vmem_limit_bytes=1024 * 1024),
    )(*results)


def solution(mesh):
    rows, slots = P("dp", "seq", None), P("dp", "seq")
    return jax.shard_map(
        on_device,
        mesh=mesh,
        in_specs=(rows, rows, P(), P(), P(), rows, slots, slots, slots, slots),
        out_specs=(slots, rows, P("seq", None), P("seq", None)),
        check_vma=False,
    )
```
